256 devices in a mesh: phase: 32 (over z_lo, y, x), lat: 8 (over z_hi, core).
Axes of the slice: x: 4, y: 4, z: 8 (z_hi: 4, z_lo: 2; z = z_hi * 2 + z_lo), core: 2. Of those that a mesh axis runs over, the one named last changes fastest.
Arguments:
- state_now: float32 [3, 256, 1024], P(None, ('lat', 'phase')), may hold values from -4 to 4
- ocean_depth: float32 [256, 1024], P('lat'), may hold values from 0.5 to 1.5
- coriolis: float32 [256], P('lat'), may hold values from -0.4 to 0.4
- phase_times: float32 [32], P('phase'), may hold values from -6 to 6
- phase_weights: float32 [32], P('phase'), may hold values from 0.003125 to 0.125
Outputs:
- state_next: float32 [3, 256, 1024], P(None, ('lat', 'phase'))
- tendency: float32 [3, 256, 1024], P(None, ('lat', 'phase'))
The draws below stay inside these ranges and needn't reach their ends.
All inputs are finite; a program needn't handle non-finite values.
Results may differ from the reference program's by a relative error of at most 0.00002.
Values sent between devices are 32-bit elements; how exact they have to be, the bound alone decides.
No kernel may reach another device: no remote copies, remote signals or barrier semaphores. Data moves between devices by JAX's collectives and lax.ppermute only.
A program may use at most 64 MiB of HBM per device.

```python
import math
import jax
import jax.numpy as jnp
from jax import lax

NLON = 1024
DEG = 8
NLAT = 256
SAMPLES = 32


def steps_of(stream_key, dims, split, least, top_value):
    factor_of, own = 1.0, jax.random.fold_in(stream_key, 6)
    for axis_at, parts in split:
        steps = jnp.exp(jax.random.uniform(jax.random.fold_in(own, axis_at), (parts,), jnp.float32, least / len(split), top_value / len(split)))
        factor_of = factor_of * jnp.repeat(steps, dims[axis_at] // parts).reshape([-1 if axis == axis_at else 1 for axis in range(len(dims))])
    return factor_of


def gaussian(stream_key, shape, deviation, most, pieces=(), held_as=jnp.bfloat16):
    level = steps_of(stream_key, shape, pieces, -0.22, 0.18) if pieces else 1.0
    array = jax.random.normal(stream_key, shape, jnp.float32) * deviation * level
    return jnp.minimum(jnp.maximum(array, -most), most).astype(held_as)


def setup_inputs(seed: int = 0) -> dict:
    streams_of = jax.random.split(jax.random.key(seed), 6)
    return {
        "state_now": gaussian(streams_of[0], (3, NLAT, NLON), 1.0, 4.0, ((1, 256),), jnp.float32),
        "ocean_depth": jnp.clip(0.5 + 1.0 * jax.random.uniform(streams_of[1], (NLAT, NLON), jnp.float32) ** steps_of(streams_of[1], (NLAT, NLON), ((0, 8),), -0.2, 0.2), 0.5, 1.5),
        "coriolis": jnp.clip(jax.random.uniform(streams_of[2], (NLAT,), jnp.float32, -0.4, 0.4) * steps_of(streams_of[2], (NLAT,), ((0, 8),), -0.4, 0.0), -0.4, 0.4),
        "phase_times": jnp.clip(jax.random.uniform(streams_of[3], (SAMPLES,), jnp.float32, -6.0, 6.0) * steps_of(streams_of[3], (SAMPLES,), ((0, 32),), -0.4, 0.0), -6.0, 6.0),
        "phase_weights": jnp.clip(jnp.exp(math.log(0.125) - 3.6888794 * jax.random.uniform(streams_of[4], (SAMPLES,), jnp.float32) ** steps_of(streams_of[4], (SAMPLES,), ((0, 32),), -0.2, 0.2)), 0.003125, 0.125),
    }


radius_scale = 2.5
time_step = 0.5
series_terms = 20


def along_lon(values):
    return (jnp.roll(values, -1, axis=-1) - jnp.roll(values, 1, axis=-1)) * 0.5


def along_lat(values):
    return (values[..., 2:, :] - values[..., :-2, :]) * 0.5


def interior(values):
    return values[..., 1:-1, :]


def wave_operator(fields, coefficients):
    height = fields[:, 0]
    eastward = fields[:, 1]
    northward = fields[:, 2]
    depth_field = coefficients[0]
    rotation = coefficients[1]
    out_height = -(along_lon(interior(depth_field * eastward)) + along_lat(depth_field * northward))
    out_east = -along_lon(interior(height)) + interior(rotation * northward)
    out_north = -along_lat(height) - interior(rotation * eastward)
    return jnp.stack([out_height, out_east, out_north], axis=1) / radius_scale


def advection(fields):
    height = fields[:, 0]
    eastward = fields[:, 1]
    northward = fields[:, 2]
    mid_east = interior(eastward)
    mid_north = interior(northward)
    out_height = -(along_lon(interior(height * eastward)) + along_lat(height * northward))
    out_east = -(mid_east * along_lon(mid_east) + mid_north * along_lat(eastward))
    out_north = -(mid_east * along_lon(mid_north) + mid_north * along_lat(northward))
    return jnp.stack([out_height, out_east, out_north], axis=1)


def series_coeffs(sample_time):
    half_time = sample_time * 0.5
    square = half_time * half_time
    result = []
    for degree in range(DEG + 1):
        summed = jnp.zeros_like(sample_time)
        term_sq = jnp.ones_like(sample_time)
        for series in range(series_terms):
            factor = (-1.0) ** series / (math.factorial(series) * math.factorial(series + degree))
            summed = summed + factor * term_sq
            term_sq = term_sq * square
        result.append(summed * half_time ** degree)
    return result


def pad_rows(values):
    return jnp.pad(values, ((0, 0), (0, 0), (1, 1), (0, 0)))


def exponential(fields, coefficients, sample_time):
    series = series_coeffs(sample_time)
    previous = fields
    accumulated = series[0] * fields
    current = wave_operator(pad_rows(fields), coefficients)
    accumulated = accumulated + 2.0 * series[1] * current
    for degree in range(2, DEG + 1):
        advanced = 2.0 * wave_operator(pad_rows(current), coefficients) + previous
        accumulated = accumulated + 2.0 * series[degree] * advanced
        previous = current
        current = advanced
    return accumulated


def averaged(state_now, coefficients, phase_times, phase_weights):
    def one_sample(summed, paired):
        sample_time, weight = paired
        waves = exponential(state_now[None], coefficients, sample_time)
        pulled = advection(pad_rows(waves))
        returned = exponential(pulled, coefficients, -sample_time)
        return summed + weight * returned[0], None

    summed, unused = lax.scan(one_sample, jnp.zeros_like(state_now), (phase_times, phase_weights))
    return summed


def reference(state_now, ocean_depth, coriolis, phase_times, phase_weights):
    stacked = jnp.stack([ocean_depth, jnp.broadcast_to(coriolis[:, None], ocean_depth.shape)])
    coefficients = jnp.pad(stacked, ((0, 0), (1, 1), (0, 0)))
    first = averaged(state_now, coefficients, phase_times, phase_weights)
    middle = state_now + time_step * first
    second = averaged(middle, coefficients, phase_times, phase_weights)
    tendency = 0.5 * (first + second)
    state_next = state_now + time_step * tendency
    return (state_next, tendency)
```

```python
import functools
import math

import jax
import jax.numpy as jnp
import numpy as np
from jax import lax
from jax.experimental import pallas as pl
from jax.experimental.pallas import tpu as pltpu
from jax.sharding import PartitionSpec as P

DEG = 8
TERMS = DEG + 1
SERIES = 20
SCALE = 2.5
STEP = 0.5

TILE = 32
LANES = 128
LEFT = 48
BASE = 36
BLOCKS = 13
PAD = 8
ROWS = PAD + 8 * BLOCKS + PAD
WIDE = 3 * LANES
SAMPLES = 32

f32 = jnp.float32
bf16 = jnp.bfloat16


def series_table():
    table = np.zeros((24, LANES), np.float32)
    for m in range(SERIES):
        for k in range(TERMS):
            table[m, k] = (-1.0) ** m / (math.factorial(m) * math.factorial(m + k))
    return table


def pack_kernel(row_ref, time_ref, weight_ref, cor_ref, state_ref, depth_ref, table_ref, out_ref, line_ref, lines_ref):
    row = row_ref[0]
    lane = lax.broadcasted_iota(jnp.int32, (1, LANES), 1)
    half = time_ref[0] * 0.5
    square = jnp.full((1, LANES), half * half, f32)
    total = jnp.zeros((1, LANES), f32)
    power = jnp.ones((1, LANES), f32)
    for m in range(SERIES):
        total = total + table_ref[m : m + 1, :] * power
        power = power * square
    scale = jnp.ones((1, LANES), f32)
    for k in range(1, TERMS):
        scale = jnp.where((lane >= k) & (lane < TERMS), scale * half, scale)
    forward = total * scale
    forward = jnp.where(lane == 0, forward, 2.0 * forward)
    backward = jnp.where(lane % 2 == 0, forward, -forward) * weight_ref[0]
    cor = jnp.full((1, LANES), cor_ref[row], f32)
    lanes = lax.broadcasted_iota(jnp.int32, (8, LANES), 1)
    mine = lax.broadcasted_iota(jnp.int32, (8, LANES), 0) == lax.rem(row, 8)
    eight = pl.ds(pl.multiple_of(lax.div(row, 8) * 8, 8), 8)
    for q in range(8):
        depth = depth_ref[eight, q * LANES : (q + 1) * LANES]
        line_ref[q : q + 1, :] = jnp.sum(jnp.where(mine, depth, 0.0), axis=0, keepdims=True)
    extras = (forward, backward, None, cor)
    for f in range(4):
        here = state_ref[f] if f < 3 else line_ref[...]
        after = pltpu.roll(here, 7, 0)
        before = pltpu.roll(here, 1, 0)
        for c in range(4):
            start = TILE * c - LEFT
            first, second = (before, here) if start < 0 else (here, after)
            shift = start % LANES
            window = jnp.where(
                lanes < LANES - shift,
                pltpu.roll(first, LANES - shift, 1),
                pltpu.roll(second, LANES - shift, 1),
            )
            if extras[f] is not None:
                window = jnp.where(lanes < TERMS, jnp.broadcast_to(extras[f], (8, LANES)), window)
            lines_ref[f, pl.ds(c, 8, stride=4), :] = window
        out_ref[:, f * LANES : (f + 1) * LANES] = lines_ref[f]


def unpack_kernel(in_ref, state_ref, next_ref, tendency_ref):
    lanes = lax.broadcasted_iota(jnp.int32, (8, LANES), 1)
    for f in range(3):
        line = jnp.zeros((8, LANES), f32)
        for c in range(4):
            piece = in_ref[pl.ds(c, 8, stride=4), :]
            shift = (TILE * (c - f)) % LANES
            if shift:
                piece = pltpu.roll(piece, shift, 1)
            line = jnp.where((lanes >= TILE * c) & (lanes < TILE * (c + 1)), piece, line)
        tendency_ref[f] = line
        next_ref[f] = state_ref[f] + STEP * line


def split(value):
    high = value.astype(bf16)
    return high, (value - high.astype(f32)).astype(bf16)


def tile_kernel(
    place_ref, own_ref, up_ref, down_ref, far_up_ref, far_down_ref, out_ref,
    p_ref, z_ref, w_ref, yh_ref, yl_ref, t_ref, depth_ref, cor_ref, mask_ref, forward_ref, backh_ref, backl_ref,
):
    lat = place_ref[0]

    def rows(block, offset=0, count=1):
        start = PAD + 8 * block + offset
        return slice(start, start + 8 * count)

    for k in range(TERMS + 1):
        p_ref[k, 0 : PAD + 8, :] = jnp.zeros((PAD + 8, WIDE), f32)
        p_ref[k, ROWS - PAD - 8 : ROWS, :] = jnp.zeros((PAD + 8, WIDE), f32)
    p_ref[TERMS] = jnp.zeros((ROWS, WIDE), f32)
    for k in range(TERMS):
        for block in (0, BLOCKS - 1):
            z_ref[k, rows(block), :] = jnp.zeros((8, WIDE), f32)
    for s in range(SAMPLES):
        for block in (0, BLOCKS - 1):
            w_ref[s, rows(block), :] = jnp.zeros((8, WIDE), f32)
    for ref in (depth_ref, cor_ref):
        ref[0 : PAD + 8, :] = jnp.zeros((PAD + 8, LANES), f32)
        ref[ROWS - PAD - 8 : ROWS, :] = jnp.zeros((PAD + 8, LANES), f32)

    def place(ref, start, count, at):
        at = PAD + BASE + at
        piece = ref[start : start + count, :]
        p_ref[0, at : at + count, :] = piece[:, :WIDE]
        depth_ref[at : at + count, :] = piece[:, WIDE:] * 0.4
        cor_ref[at : at + count, :] = jnp.broadcast_to(piece[:, WIDE : WIDE + 1] * 0.8, (count, LANES))

    place(own_ref, 0, TILE, 0)
    place(up_ref, 0, TILE, -TILE)
    place(down_ref, 0, TILE, TILE)
    place(far_up_ref, 6, 2, -TILE - 2)
    place(far_down_ref, 0, 2, 2 * TILE)

    at_row = lax.broadcasted_iota(jnp.int32, (ROWS, LANES), 0) + (TILE * lat - BASE - PAD)
    mask_ref[...] = jnp.where((at_row >= 0) & (at_row < 8 * TILE), 1.0, 0.0).astype(f32)

    term = lax.broadcasted_iota(jnp.int32, (LANES, 256), 0)
    column = lax.broadcasted_iota(jnp.int32, (LANES, 256), 1)
    group = column // 8
    high_at = (group == term) | (group - 10 == term)
    low_at = group - 20 == term
    pick_high = jnp.where(high_at & (term < TERMS), 1.0, 0.0).astype(bf16)
    pick_low = jnp.where(low_at & (term < TERMS), 1.0, 0.0).astype(bf16)
    same = lax.broadcasted_iota(jnp.int32, (256, 256), 0) % 8 == lax.broadcasted_iota(jnp.int32, (256, 256), 1) % 8

    def spread(block):
        value = own_ref[:, block * LANES : (block + 1) * LANES]
        return split(jnp.broadcast_to(value[:, None, :], (SAMPLES, 8, LANES)).reshape(256, LANES))

    def picked(value, pick):
        return jnp.dot(value, pick, preferred_element_type=f32)

    high, low = spread(0)
    forward = picked(high, pick_high) + picked(low, pick_low)
    forward_ref[...] = jnp.where(same, forward, 0.0).astype(bf16)
    high, low = spread(1)
    pick = jnp.where((group == term) & (term < TERMS), 1.0, 0.0).astype(bf16)[:, :LANES]
    back_high = jnp.where(same[:, :LANES], picked(high, pick), 0.0).T
    back_low = jnp.where(same[:, :LANES], picked(low, pick), 0.0).T
    backh_ref[0:80, :] = back_high[0:80].astype(bf16)
    backh_ref[80:160, :] = back_low[0:80].astype(bf16)
    backl_ref[...] = back_high[0:80].astype(bf16)

    def east(value):
        return pltpu.roll(value, LANES - 1, 1) - pltpu.roll(value, 1, 1)

    def operator(ref, k, block):
        mid, up, down = rows(block), rows(block, 1), rows(block, -1)
        h_at, u_at, v_at = slice(0, LANES), slice(LANES, 2 * LANES), slice(2 * LANES, WIDE)
        h, u, v = ref[k, mid, h_at], ref[k, mid, u_at], ref[k, mid, v_at]
        mask, cor = mask_ref[mid, :], cor_ref[mid, :]
        flux = east(depth_ref[mid, :] * u) + (depth_ref[up, :] * ref[k, up, v_at] - depth_ref[down, :] * ref[k, down, v_at])
        out_h = -(mask * flux)
        out_u = cor * v - 0.4 * east(h)
        out_v = mask * (-0.4 * (ref[k, up, h_at] - ref[k, down, h_at])) - cor * u
        return out_h, out_u, out_v

    def fields(ref, k, block):
        return [ref[k, rows(block), f * LANES : (f + 1) * LANES] for f in range(3)]

    def store(ref, k, block, values):
        for f in range(3):
            ref[k, rows(block), f * LANES : (f + 1) * LANES] = values[f]

    def averaged(outer, inner):
        for k in range(1, TERMS):
            for block in range(*outer):
                new = operator(p_ref, k - 1, block)
                if k == 1:
                    new = [0.5 * value for value in new]
                else:
                    new = [a + b for a, b in zip(new, fields(p_ref, k - 2, block))]
                store(p_ref, k, block, new)

        first, last = inner
        for block in range(first, last):
            value = p_ref[:, rows(block), :].reshape(80, WIDE)
            high, low = split(value)
            stacked = jnp.concatenate([high, low, high, jnp.zeros((16, WIDE), bf16)], axis=0)
            waves = jnp.dot(forward_ref[...], stacked, preferred_element_type=f32)
            w_ref[:, rows(block), :] = waves.reshape(SAMPLES, 8, WIDE)

        def advect(s, block):
            mid, up, down = rows(block), rows(block, 1), rows(block, -1)
            h_at, u_at, v_at = slice(0, LANES), slice(LANES, 2 * LANES), slice(2 * LANES, WIDE)
            h, u, v = w_ref[s, mid, h_at], w_ref[s, mid, u_at], w_ref[s, mid, v_at]
            v_up, v_down = w_ref[s, up, v_at], w_ref[s, down, v_at]
            out_h = east(h * u) + (w_ref[s, up, h_at] * v_up - w_ref[s, down, h_at] * v_down)
            out_u = u * east(u) + v * (w_ref[s, up, u_at] - w_ref[s, down, u_at])
            out_v = u * east(v) + v * (v_up - v_down)
            return out_h, out_u, out_v

        def pair(n, carry):
            for block in range(first, last):
                one, two = advect(2 * n, block), advect(2 * n + 1, block)
                for f in range(3):
                    high, low = split(jnp.concatenate([one[f], two[f]], axis=0))
                    yh_ref[block, n, :, f * LANES : (f + 1) * LANES] = high
                    yl_ref[block, n, :, f * LANES : (f + 1) * LANES] = low
            return carry

        lax.fori_loop(0, SAMPLES // 2, pair, 0)

        for block in range(first, last):
            high = yh_ref[block].reshape(256, WIDE)
            low = yl_ref[block].reshape(256, WIDE)
            both = jnp.dot(backh_ref[...], high, preferred_element_type=f32)
            total = both[0:80] + both[80:160] + jnp.dot(backl_ref[...], low, preferred_element_type=f32)
            total = total * -0.5
            for k in range(TERMS):
                term_at = total[8 * k : 8 * k + 8]
                z_ref[k, rows(block), 0:LANES] = term_at[:, 0:LANES] * mask_ref[rows(block), :]
                z_ref[k, rows(block), LANES:WIDE] = term_at[:, LANES:WIDE]

        for k in range(DEG - 1, -1, -1):
            for block in range(first, last):
                new = operator(z_ref, k + 1, block)
                if k == 0:
                    new = [0.5 * value for value in new]
                new = [a + b for a, b in zip(new, fields(z_ref, k, block))]
                if k + 2 < TERMS:
                    new = [a + b for a, b in zip(new, fields(z_ref, k + 2, block))]
                store(z_ref, k, block, new)

    averaged((0, 13), (1, 12))
    for block in range(2, 11):
        at = rows(block)
        t_ref[at, :] = z_ref[0, at, :]
        p_ref[0, at, :] = p_ref[0, at, :] + STEP * z_ref[0, at, :]
    averaged((2, 11), (3, 10))
    at = slice(PAD + BASE, PAD + BASE + TILE)
    tendency = 0.5 * (t_ref[at, :] + z_ref[0, at, :])
    lanes = lax.broadcasted_iota(jnp.int32, (TILE, LANES), 1)
    parts = [pltpu.roll(tendency[:, f * LANES : (f + 1) * LANES], (TILE * f - LEFT) % LANES, 1) for f in range(3)]
    out_ref[...] = jnp.where(lanes < TILE, parts[0], jnp.where(lanes < 2 * TILE, parts[1], parts[2]))


def vmem():
    return pl.BlockSpec(memory_space=pltpu.VMEM)


def smem():
    return pl.BlockSpec(memory_space=pltpu.SMEM)


def pack(row, times, weights, cor, state, depth):
    return pl.pallas_call(
        pack_kernel,
        out_shape=jax.ShapeDtypeStruct((TILE, 4 * LANES), f32),
        in_specs=[smem(), smem(), smem(), smem(), vmem(), vmem(), vmem()],
        out_specs=vmem(),
        scratch_shapes=[pltpu.VMEM((8, LANES), f32), pltpu.VMEM((4, TILE, LANES), f32)],
        name="pack",
    )(row, times, weights, cor, state, depth, jnp.asarray(series_table()))


def tile(place, own, up, down, far_up, far_down):
    return pl.pallas_call(
        tile_kernel,
        out_shape=jax.ShapeDtypeStruct((TILE, LANES), f32),
        in_specs=[smem()] + [vmem()] * 5,
        out_specs=vmem(),
        scratch_shapes=[
            pltpu.VMEM((TERMS + 1, ROWS, WIDE), f32),
            pltpu.VMEM((TERMS, ROWS, WIDE), f32),
            pltpu.VMEM((SAMPLES, ROWS, WIDE), f32),
            pltpu.VMEM((BLOCKS, SAMPLES // 2, 16, WIDE), bf16),
            pltpu.VMEM((BLOCKS, SAMPLES // 2, 16, WIDE), bf16),
            pltpu.VMEM((ROWS, WIDE), f32),
            pltpu.VMEM((ROWS, LANES), f32),
            pltpu.VMEM((ROWS, LANES), f32),
            pltpu.VMEM((ROWS, LANES), f32),
            pltpu.VMEM((256, 256), bf16),
            pltpu.VMEM((160, 256), bf16),
            pltpu.VMEM((80, 256), bf16),
        ],
        compiler_params=pltpu.CompilerParams(vmem_limit_bytes=48 * 1024 * 1024),
        name="tile",
    )(place, own, up, down, far_up, far_down)


def unpack(columns, state):
    shape = jax.ShapeDtypeStruct((3, 8, LANES), f32)
    return pl.pallas_call(
        unpack_kernel,
        out_shape=(shape, shape),
        in_specs=[vmem(), vmem()],
        out_specs=(vmem(), vmem()),
        name="unpack",
    )(columns, state)


def per_device(tiles, state_now, ocean_depth, coriolis, phase_times, phase_weights):
    state = state_now.reshape(3, 8, LANES)
    row = lax.axis_index("phase").astype(jnp.int32)[None]
    lat = lax.axis_index("lat").astype(jnp.int32)[None]
    message = pack(row, phase_times, phase_weights, coriolis, state, ocean_depth)
    own = lax.all_to_all(message, "phase", 0, 0, tiled=True)
    up = lax.ppermute(own, "lat", [(i, i + 1) for i in range(tiles - 1)])
    down = lax.ppermute(own, "lat", [(i + 1, i) for i in range(tiles - 1)])
    far_up = lax.ppermute(own[TILE - 8 :], "lat", [(i, i + 2) for i in range(tiles - 2)])
    far_down = lax.ppermute(own[:8], "lat", [(i + 2, i) for i in range(tiles - 2)])
    columns = tile(lat, own, up, down, far_up, far_down)
    columns = lax.all_to_all(columns, "phase", 0, 0, tiled=True)
    state_next, tendency = unpack(columns, state)
    return state_next.reshape(state_now.shape), tendency.reshape(state_now.shape)


def solution(mesh):
    rows = P(None, ("lat", "phase"), None)
    return jax.shard_map(
        functools.partial(per_device, mesh.shape["lat"]),
        mesh=mesh,
        in_specs=(rows, P("lat", None), P("lat"), P("phase"), P("phase")),
        out_specs=(rows, rows),
        check_vma=False,
    )
```

```python
import functools
import math

import jax
import jax.numpy as jnp
import numpy as np
from jax import lax
from jax.experimental import pallas as pl
from jax.experimental.pallas import tpu as pltpu
from jax.sharding import PartitionSpec as P

DEG = 8
TERMS = DEG + 1
SERIES = 20
SCALE = 2.5
STEP = 0.5
NLON = 1024

TILE = 32
LANES = 128
LEFT = 48
BASE = 36
BLOCKS = 13
PAD = 8
ROWS = PAD + 8 * BLOCKS + PAD
WIDE = 3 * LANES
SAMPLES = 32

f32 = jnp.float32
bf16 = jnp.bfloat16


def series_table():
    table = np.zeros((24, LANES), np.float32)
    for m in range(SERIES):
        for k in range(TERMS):
            table[m, k] = (-1.0) ** m / (math.factorial(m) * math.factorial(m + k))
    return table


def pack_kernel(row_ref, time_ref, weight_ref, cor_ref, state_ref, depth_ref, table_ref, out_ref, line_ref):
    row = row_ref[0]
    lane = lax.broadcasted_iota(jnp.int32, (1, LANES), 1)
    half = time_ref[0] * 0.5
    square = jnp.full((1, LANES), half * half, f32)
    total = jnp.zeros((1, LANES), f32)
    power = jnp.ones((1, LANES), f32)
    for m in range(SERIES):
        total = total + table_ref[m : m + 1, :] * power
        power = power * square
    scale = jnp.ones((1, LANES), f32)
    for k in range(1, TERMS):
        scale = jnp.where((lane >= k) & (lane < TERMS), scale * half, scale)
    forward = total * scale
    forward = jnp.where(lane == 0, forward, 2.0 * forward)
    backward = jnp.where(lane % 2 == 0, forward, -forward) * weight_ref[0]
    cor = jnp.full((1, LANES), cor_ref[row], f32)
    lanes = lax.broadcasted_iota(jnp.int32, (8, LANES), 1)
    mine = lax.broadcasted_iota(jnp.int32, (8, LANES), 0) == lax.rem(row, 8)
    for q in range(8):
        depth = depth_ref[:, q * LANES : (q + 1) * LANES]
        line_ref[q : q + 1, :] = jnp.sum(jnp.where(mine, depth, 0.0), axis=0, keepdims=True)
    extras = (forward, backward, None, cor)
    for f in range(4):
        here = state_ref[f] if f < 3 else line_ref[...]
        after = pltpu.roll(here, 7, 0)
        before = pltpu.roll(here, 1, 0)
        for c in range(4):
            start = TILE * c - LEFT
            first, second = (before, here) if start < 0 else (here, after)
            shift = start % LANES
            window = jnp.where(
                lanes < LANES - shift,
                pltpu.roll(first, LANES - shift, 1),
                pltpu.roll(second, LANES - shift, 1),
            )
            if extras[f] is not None:
                window = jnp.where(lanes < TERMS, jnp.broadcast_to(extras[f], (8, LANES)), window)
            for core in range(2):
                out_ref[pl.ds(4 * (TILE * core + c) + f, 8, stride=16), :] = window


def unpack_kernel(in_ref, state_ref, next_ref, tendency_ref):
    lanes = lax.broadcasted_iota(jnp.int32, (8, LANES), 1)
    for f in range(3):
        line = jnp.zeros((8, LANES), f32)
        for c in range(4):
            piece = in_ref[pl.ds(c, 8, stride=4), :]
            shift = (TILE * (c - f)) % LANES
            if shift:
                piece = pltpu.roll(piece, shift, 1)
            line = jnp.where((lanes >= TILE * c) & (lanes < TILE * (c + 1)), piece, line)
        tendency_ref[f] = line
        next_ref[f] = state_ref[f] + STEP * line


def split(value):
    high = value.astype(bf16)
    return high, (value - high.astype(f32)).astype(bf16)


def tile_kernel(
    place_ref, own_ref, near_ref, far_ref, out_ref,
    p_ref, z_ref, w_ref, yh_ref, yl_ref, t_ref, depth_ref, cor_ref, mask_ref, forward_ref, backh_ref, backl_ref,
):
    lat = place_ref[0]
    core = lax.rem(lat, 2)

    def rows(block, offset=0, count=1):
        start = PAD + 8 * block + offset
        return slice(start, start + 8 * count)

    for k in range(TERMS + 1):
        p_ref[k, 0 : PAD + 8, :] = jnp.zeros((PAD + 8, WIDE), f32)
        p_ref[k, ROWS - PAD - 8 : ROWS, :] = jnp.zeros((PAD + 8, WIDE), f32)
    p_ref[TERMS] = jnp.zeros((ROWS, WIDE), f32)
    for k in range(TERMS):
        for block in (0, BLOCKS - 1):
            z_ref[k, rows(block), :] = jnp.zeros((8, WIDE), f32)
    for s in range(SAMPLES):
        for block in (0, BLOCKS - 1):
            w_ref[s, rows(block), :] = jnp.zeros((8, WIDE), f32)
    for ref in (depth_ref, cor_ref):
        ref[0 : PAD + 8, :] = jnp.zeros((PAD + 8, LANES), f32)
        ref[ROWS - PAD - 8 : ROWS, :] = jnp.zeros((PAD + 8, LANES), f32)

    def place(ref, count, at):
        at = PAD + BASE + at
        h, u, v, depth, = [ref[pl.ds(f, count, stride=4), :] for f in range(4)]
        p_ref[0, at : at + count, 0:LANES] = h
        p_ref[0, at : at + count, LANES : 2 * LANES] = u
        p_ref[0, at : at + count, 2 * LANES : WIDE] = v
        depth_ref[at : at + count, :] = depth * 0.4
        cor_ref[at : at + count, :] = jnp.broadcast_to(depth[:, 0:1] * 0.8, (count, LANES))

    @pl.when(core == 0)
    def _():
        place(own_ref, 2 * TILE, 0)
        place(near_ref, TILE + 2, -TILE - 2)
        place(far_ref, 2, 2 * TILE)

    @pl.when(core == 1)
    def _():
        place(own_ref, 2 * TILE, -TILE)
        place(near_ref, TILE + 2, TILE)
        place(far_ref, 2, -TILE - 2)

    at_row = lax.broadcasted_iota(jnp.int32, (ROWS, LANES), 0) + (TILE * lat - BASE - PAD)
    mask_ref[...] = jnp.where((at_row >= 0) & (at_row < 8 * TILE), 1.0, 0.0).astype(f32)

    term = lax.broadcasted_iota(jnp.int32, (LANES, 256), 0)
    column = lax.broadcasted_iota(jnp.int32, (LANES, 256), 1)
    group = column // 8
    high_at = (group == term) | (group - 10 == term)
    low_at = group - 20 == term
    pick_high = jnp.where(high_at & (term < TERMS), 1.0, 0.0).astype(bf16)
    pick_low = jnp.where(low_at & (term < TERMS), 1.0, 0.0).astype(bf16)
    same = lax.broadcasted_iota(jnp.int32, (256, 256), 0) % 8 == lax.broadcasted_iota(jnp.int32, (256, 256), 1) % 8

    def spread(block):
        value = own_ref[pl.ds(block, SAMPLES, stride=4), :]
        return split(jnp.broadcast_to(value[:, None, :], (SAMPLES, 8, LANES)).reshape(256, LANES))

    def picked(value, pick):
        return jnp.dot(value, pick, preferred_element_type=f32)

    high, low = spread(0)
    forward = picked(high, pick_high) + picked(low, pick_low)
    forward_ref[...] = jnp.where(same, forward, 0.0).astype(bf16)
    high, low = spread(1)
    pick = jnp.where((group == term) & (term < TERMS), 1.0, 0.0).astype(bf16)[:, :LANES]
    back_high = jnp.where(same[:, :LANES], picked(high, pick), 0.0).T
    back_low = jnp.where(same[:, :LANES], picked(low, pick), 0.0).T
    backh_ref[0:80, :] = back_high[0:80].astype(bf16)
    backh_ref[80:160, :] = back_low[0:80].astype(bf16)
    backl_ref[...] = back_high[0:80].astype(bf16)

    def east(value):
        return pltpu.roll(value, LANES - 1, 1) - pltpu.roll(value, 1, 1)

    def operator(ref, k, block):
        mid, up, down = rows(block), rows(block, 1), rows(block, -1)
        h_at, u_at, v_at = slice(0, LANES), slice(LANES, 2 * LANES), slice(2 * LANES, WIDE)
        h, u, v = ref[k, mid, h_at], ref[k, mid, u_at], ref[k, mid, v_at]
        mask, cor = mask_ref[mid, :], cor_ref[mid, :]
        flux = east(depth_ref[mid, :] * u) + (depth_ref[up, :] * ref[k, up, v_at] - depth_ref[down, :] * ref[k, down, v_at])
        out_h = -(mask * flux)
        out_u = cor * v - 0.4 * east(h)
        out_v = mask * (-0.4 * (ref[k, up, h_at] - ref[k, down, h_at])) - cor * u
        return out_h, out_u, out_v

    def fields(ref, k, block):
        return [ref[k, rows(block), f * LANES : (f + 1) * LANES] for f in range(3)]

    def store(ref, k, block, values):
        for f in range(3):
            ref[k, rows(block), f * LANES : (f + 1) * LANES] = values[f]

    def averaged(outer, inner):
        for k in range(1, TERMS):
            for block in range(*outer):
                new = operator(p_ref, k - 1, block)
                if k == 1:
                    new = [0.5 * value for value in new]
                else:
                    new = [a + b for a, b in zip(new, fields(p_ref, k - 2, block))]
                store(p_ref, k, block, new)

        first, last = inner
        for block in range(first, last):
            value = p_ref[:, rows(block), :].reshape(80, WIDE)
            high, low = split(value)
            stacked = jnp.concatenate([high, low, high, jnp.zeros((16, WIDE), bf16)], axis=0)
            waves = jnp.dot(forward_ref[...], stacked, preferred_element_type=f32)
            w_ref[:, rows(block), :] = waves.reshape(SAMPLES, 8, WIDE)

        def advect(s, block):
            mid, up, down = rows(block), rows(block, 1), rows(block, -1)
            h_at, u_at, v_at = slice(0, LANES), slice(LANES, 2 * LANES), slice(2 * LANES, WIDE)
            h, u, v = w_ref[s, mid, h_at], w_ref[s, mid, u_at], w_ref[s, mid, v_at]
            v_up, v_down = w_ref[s, up, v_at], w_ref[s, down, v_at]
            out_h = east(h * u) + (w_ref[s, up, h_at] * v_up - w_ref[s, down, h_at] * v_down)
            out_u = u * east(u) + v * (w_ref[s, up, u_at] - w_ref[s, down, u_at])
            out_v = u * east(v) + v * (v_up - v_down)
            return out_h, out_u, out_v

        def pair(n, carry):
            for block in range(first, last):
                one, two = advect(2 * n, block), advect(2 * n + 1, block)
                for f in range(3):
                    high, low = split(jnp.concatenate([one[f], two[f]], axis=0))
                    yh_ref[block, n, :, f * LANES : (f + 1) * LANES] = high
                    yl_ref[block, n, :, f * LANES : (f + 1) * LANES] = low
            return carry

        lax.fori_loop(0, SAMPLES // 2, pair, 0)

        for block in range(first, last):
            high = yh_ref[block].reshape(256, WIDE)
            low = yl_ref[block].reshape(256, WIDE)
            both = jnp.dot(backh_ref[...], high, preferred_element_type=f32)
            total = both[0:80] + both[80:160] + jnp.dot(backl_ref[...], low, preferred_element_type=f32)
            total = total * -0.5
            for k in range(TERMS):
                term_at = total[8 * k : 8 * k + 8]
                z_ref[k, rows(block), 0:LANES] = term_at[:, 0:LANES] * mask_ref[rows(block), :]
                z_ref[k, rows(block), LANES:WIDE] = term_at[:, LANES:WIDE]

        for k in range(DEG - 1, -1, -1):
            for block in range(first, last):
                new = operator(z_ref, k + 1, block)
                if k == 0:
                    new = [0.5 * value for value in new]
                new = [a + b for a, b in zip(new, fields(z_ref, k, block))]
                if k + 2 < TERMS:
                    new = [a + b for a, b in zip(new, fields(z_ref, k + 2, block))]
                store(z_ref, k, block, new)

    averaged((0, 13), (1, 12))
    for block in range(2, 11):
        at = rows(block)
        t_ref[at, :] = z_ref[0, at, :]
        p_ref[0, at, :] = p_ref[0, at, :] + STEP * z_ref[0, at, :]
    averaged((2, 11), (3, 10))
    at = slice(PAD + BASE, PAD + BASE + TILE)
    tendency = 0.5 * (t_ref[at, :] + z_ref[0, at, :])
    lanes = lax.broadcasted_iota(jnp.int32, (TILE, LANES), 1)
    parts = [pltpu.roll(tendency[:, f * LANES : (f + 1) * LANES], (TILE * f - LEFT) % LANES, 1) for f in range(3)]
    out_ref[...] = jnp.where(lanes < TILE, parts[0], jnp.where(lanes < 2 * TILE, parts[1], parts[2]))


def vmem():
    return pl.BlockSpec(memory_space=pltpu.VMEM)


def smem():
    return pl.BlockSpec(memory_space=pltpu.SMEM)


def pack(row, times, weights, cor, state, depth):
    grid = pltpu.PrefetchScalarGridSpec(
        num_scalar_prefetch=1,
        grid=(1,),
        in_specs=[
            smem(), smem(), smem(), vmem(),
            pl.BlockSpec((8, NLON), lambda i, at: (lax.div(at[0], 8), 0)),
            vmem(),
        ],
        out_specs=vmem(),
        scratch_shapes=[pltpu.VMEM((8, LANES), f32)],
    )
    return pl.pallas_call(
        pack_kernel,
        out_shape=jax.ShapeDtypeStruct((2 * TILE * 4, LANES), f32),
        grid_spec=grid,
        name="pack",
    )(row, times, weights, cor, state, depth, jnp.asarray(series_table()))


def tile(place, own, near, far):
    return pl.pallas_call(
        tile_kernel,
        out_shape=jax.ShapeDtypeStruct((TILE, LANES), f32),
        in_specs=[smem()] + [vmem()] * 3,
        out_specs=vmem(),
        scratch_shapes=[
            pltpu.VMEM((TERMS + 1, ROWS, WIDE), f32),
            pltpu.VMEM((TERMS, ROWS, WIDE), f32),
            pltpu.VMEM((SAMPLES, ROWS, WIDE), f32),
            pltpu.VMEM((BLOCKS, SAMPLES // 2, 16, WIDE), bf16),
            pltpu.VMEM((BLOCKS, SAMPLES // 2, 16, WIDE), bf16),
            pltpu.VMEM((ROWS, WIDE), f32),
            pltpu.VMEM((ROWS, LANES), f32),
            pltpu.VMEM((ROWS, LANES), f32),
            pltpu.VMEM((ROWS, LANES), f32),
            pltpu.VMEM((256, 256), bf16),
            pltpu.VMEM((160, 256), bf16),
            pltpu.VMEM((80, 256), bf16),
        ],
        compiler_params=pltpu.CompilerParams(vmem_limit_bytes=48 * 1024 * 1024),
        name="tile",
    )(place, own, near, far)


def unpack(columns, state):
    shape = jax.ShapeDtypeStruct((3, 8, LANES), f32)
    return pl.pallas_call(
        unpack_kernel,
        out_shape=(shape, shape),
        in_specs=[vmem(), vmem()],
        out_specs=(vmem(), vmem()),
        name="unpack",
    )(columns, state)


def per_device(ring, state_now, ocean_depth, coriolis, phase_times, phase_weights):
    state = state_now.reshape(3, 8, LANES)
    row = lax.axis_index("phase").astype(jnp.int32)
    core = lax.axis_index("core").astype(jnp.int32)
    lat = 2 * lax.axis_index("ring").astype(jnp.int32) + core
    message = pack(row[None], phase_times, phase_weights, coriolis, state, ocean_depth)
    own = lax.all_to_all(message, ("core", "phase"), 0, 0, tiled=True)
    devices = ("phase", "ring", "core")

    def index(phase, at, of):
        return (phase * ring + at) * 2 + of

    def pairs(step):
        moves = [(at, at + step, 0) for at in range(ring)] + [(at, at - step, 1) for at in range(ring)]
        return [(index(p, a, c), index(p, b, c)) for p in range(TILE) for a, b, c in moves if 0 <= b < ring]

    near = lax.dynamic_slice_in_dim(own, jnp.where(core == 0, 4 * (TILE - 2), 0), 4 * (TILE + 2), 0)
    far = lax.dynamic_slice_in_dim(own, jnp.where(core == 0, 0, 4 * (2 * TILE - 2)), 8, 0)
    near = lax.ppermute(near, devices, pairs(1))
    far = lax.ppermute(far, devices, pairs(-1))
    columns = tile(lat[None], own, near, far)
    columns = lax.all_to_all(columns, "phase", 0, 0, tiled=True)
    state_next, tendency = unpack(columns, state)
    return state_next.reshape(state_now.shape), tendency.reshape(state_now.shape)


def solution(mesh):
    phase, lat = mesh.shape["phase"], mesh.shape["lat"]
    mesh = jax.sharding.Mesh(mesh.devices.reshape(phase, lat // 2, 2), ("phase", "ring", "core"))
    rows = P(None, ("ring", "core", "phase"), None)
    return jax.shard_map(
        functools.partial(per_device, lat // 2),
        mesh=mesh,
        in_specs=(rows, P(("ring", "core"), None), P(("ring", "core")), P("phase"), P("phase")),
        out_specs=(rows, rows),
        check_vma=False,
    )
```

```python
import functools
import math

import jax
import jax.numpy as jnp
import numpy as np
from jax import lax
from jax.experimental import pallas as pl
from jax.experimental.pallas import tpu as pltpu
from jax.sharding import PartitionSpec as P

DEG = 8
TERMS = DEG + 1
SERIES = 20
SCALE = 2.5
STEP = 0.5
NLON = 1024

TILE = 32
LANES = 128
LEFT = 48
BASE = 36
BLOCKS = 13
PAD = 8
ROWS = PAD + 8 * BLOCKS + PAD
WIDE = 3 * LANES
EXTRA = False
PIPELINED = True
SENT = 5 * LANES if EXTRA else WIDE
W_ROWS = 8 * 9 + 16
TILE_SHAPES = [(256, 128), (136, 128), (8, 128)]
SAMPLES = 32

f32 = jnp.float32
bf16 = jnp.bfloat16


def series_table():
    table = np.zeros((24, LANES), np.float32)
    for m in range(SERIES):
        for k in range(TERMS):
            table[m, k] = (-1.0) ** m / (math.factorial(m) * math.factorial(m + k))
    return table


def pack_kernel(row_ref, time_ref, weight_ref, cor_ref, state_ref, depth_ref, table_ref, out_ref, line_ref):
    row = row_ref[0]
    lane = lax.broadcasted_iota(jnp.int32, (1, LANES), 1)
    half = time_ref[0] * 0.5
    square = jnp.full((1, LANES), half * half, f32)
    total = jnp.zeros((1, LANES), f32)
    power = jnp.ones((1, LANES), f32)
    for m in range(SERIES):
        total = total + table_ref[m : m + 1, :] * power
        power = power * square
    scale = jnp.ones((1, LANES), f32)
    for k in range(1, TERMS):
        scale = jnp.where((lane >= k) & (lane < TERMS), scale * half, scale)
    forward = total * scale
    forward = jnp.where(lane == 0, forward, 2.0 * forward)
    backward = jnp.where(lane % 2 == 0, forward, -forward) * weight_ref[0]
    cor = jnp.full((1, LANES), cor_ref[row], f32)
    lanes = lax.broadcasted_iota(jnp.int32, (8, LANES), 1)
    mine = lax.broadcasted_iota(jnp.int32, (8, LANES), 0) == lax.rem(row, 8)
    for q in range(8):
        depth = depth_ref[:, q * LANES : (q + 1) * LANES]
        line_ref[q : q + 1, :] = jnp.sum(jnp.where(mine, depth, 0.0), axis=0, keepdims=True)
    extras = (forward, backward, None, cor)
    for f in range(4):
        here = state_ref[f] if f < 3 else line_ref[...]
        after = pltpu.roll(here, 7, 0)
        before = pltpu.roll(here, 1, 0)
        for c in range(4):
            start = TILE * c - LEFT
            first, second = (before, here) if start < 0 else (here, after)
            shift = start % LANES
            window = jnp.where(
                lanes < LANES - shift,
                pltpu.roll(first, LANES - shift, 1),
                pltpu.roll(second, LANES - shift, 1),
            )
            if extras[f] is not None:
                window = jnp.where(lanes < TERMS, jnp.broadcast_to(extras[f], (8, LANES)), window)
            for core in range(2):
                out_ref[pl.ds(4 * (TILE * core + c) + f, 8, stride=16), :] = window


def unpack_kernel(in_ref, state_ref, next_ref, tendency_ref):
    lanes = lax.broadcasted_iota(jnp.int32, (8, LANES), 1)
    for f in range(3):
        line = jnp.zeros((8, LANES), f32)
        for c in range(4):
            piece = in_ref[pl.ds(c, 8, stride=4), :]
            shift = (TILE * (c - f)) % LANES
            if shift:
                piece = pltpu.roll(piece, shift, 1)
            line = jnp.where((lanes >= TILE * c) & (lanes < TILE * (c + 1)), piece, line)
        tendency_ref[f] = line
        next_ref[f] = state_ref[f] + STEP * line


def split(value):
    high = value.astype(bf16)
    return high, (value - high.astype(f32)).astype(bf16)


def tile_kernel(
    place_ref, own_ref, near_ref, far_ref, out_ref,
    p_ref, z_ref, w_ref, yh_ref, yl_ref, t_ref, depth_ref, cor_ref, mask_ref, forward_ref, backh_ref, backl_ref,
):
    lat = place_ref[0]
    core = lax.rem(lat, 2)

    def rows(block, offset=0, count=1):
        start = PAD + 8 * block + offset
        return slice(start, start + 8 * count)

    for k in range(TERMS + 1):
        p_ref[k, 0 : PAD + 8, :] = jnp.zeros((PAD + 8, WIDE), f32)
        p_ref[k, ROWS - PAD - 8 : ROWS, :] = jnp.zeros((PAD + 8, WIDE), f32)
    p_ref[TERMS] = jnp.zeros((ROWS, WIDE), f32)
    for k in range(TERMS):
        z_ref[k, 0 : PAD + 16, :] = jnp.zeros((PAD + 16, WIDE), f32)
        z_ref[k, ROWS - PAD - 16 : ROWS, :] = jnp.zeros((PAD + 16, WIDE), f32)
    for s in range(SAMPLES):
        w_ref[s, 0:8, :] = jnp.zeros((8, SENT), f32)
        w_ref[s, W_ROWS - 8 : W_ROWS, :] = jnp.zeros((8, SENT), f32)
    for ref in (depth_ref, cor_ref):
        ref[0 : PAD + 8, :] = jnp.zeros((PAD + 8, LANES), f32)
        ref[ROWS - PAD - 8 : ROWS, :] = jnp.zeros((PAD + 8, LANES), f32)

    def place(ref, count, at):
        at = PAD + BASE + at
        h, u, v, depth, = [ref[pl.ds(f, count, stride=4), :] for f in range(4)]
        p_ref[0, at : at + count, 0:LANES] = h
        p_ref[0, at : at + count, LANES : 2 * LANES] = u
        p_ref[0, at : at + count, 2 * LANES : WIDE] = v
        depth_ref[at : at + count, :] = depth * 0.4
        cor_ref[at : at + count, :] = jnp.broadcast_to(depth[:, 0:1] * 0.8, (count, LANES))

    @pl.when(core == 0)
    def _():
        place(own_ref, 2 * TILE, 0)
        place(near_ref, TILE + 2, -TILE - 2)
        place(far_ref, 2, 2 * TILE)

    @pl.when(core == 1)
    def _():
        place(own_ref, 2 * TILE, -TILE)
        place(near_ref, TILE + 2, TILE)
        place(far_ref, 2, -TILE - 2)

    at_row = lax.broadcasted_iota(jnp.int32, (ROWS, LANES), 0) + (TILE * lat - BASE - PAD)
    mask_ref[...] = jnp.where((at_row >= 0) & (at_row < 8 * TILE), 1.0, 0.0).astype(f32)

    term = lax.broadcasted_iota(jnp.int32, (LANES, 256), 0)
    column = lax.broadcasted_iota(jnp.int32, (LANES, 256), 1)
    group = column // 8
    high_at = (group == term) | (group - 10 == term)
    low_at = group - 20 == term
    pick_high = jnp.where(high_at & (term < TERMS), 1.0, 0.0).astype(bf16)
    pick_low = jnp.where(low_at & (term < TERMS), 1.0, 0.0).astype(bf16)
    same = lax.broadcasted_iota(jnp.int32, (256, 256), 0) % 8 == lax.broadcasted_iota(jnp.int32, (256, 256), 1) % 8

    def spread(block):
        value = own_ref[pl.ds(block, SAMPLES, stride=4), :]
        return split(jnp.broadcast_to(value[:, None, :], (SAMPLES, 8, LANES)).reshape(256, LANES))

    def picked(value, pick):
        return jnp.dot(value, pick, preferred_element_type=f32)

    high, low = spread(0)
    forward = picked(high, pick_high) + picked(low, pick_low)
    forward_ref[...] = jnp.where(same, forward, 0.0).astype(bf16)
    high, low = spread(1)
    pick = jnp.where((group == term) & (term < TERMS), 1.0, 0.0).astype(bf16)[:, :LANES]
    back_high = jnp.where(same[:, :LANES], picked(high, pick), 0.0).T
    back_low = jnp.where(same[:, :LANES], picked(low, pick), 0.0).T
    backh_ref[0:80, :] = back_high[0:80].astype(bf16)
    backh_ref[80:160, :] = back_low[0:80].astype(bf16)
    backl_ref[...] = back_high[0:80].astype(bf16)

    def east(value):
        return pltpu.roll(value, LANES - 1, 1) - pltpu.roll(value, 1, 1)

    def operator(ref, k, block):
        mid, up, down = rows(block), rows(block, 1), rows(block, -1)
        h_at, u_at, v_at = slice(0, LANES), slice(LANES, 2 * LANES), slice(2 * LANES, WIDE)
        h, u, v = ref[k, mid, h_at], ref[k, mid, u_at], ref[k, mid, v_at]
        mask, cor = mask_ref[mid, :], cor_ref[mid, :]
        flux = east(depth_ref[mid, :] * u) + (depth_ref[up, :] * ref[k, up, v_at] - depth_ref[down, :] * ref[k, down, v_at])
        out_h = -(mask * flux)
        out_u = cor * v - 0.4 * east(h)
        out_v = mask * (-0.4 * (ref[k, up, h_at] - ref[k, down, h_at])) - cor * u
        return out_h, out_u, out_v

    def fields(ref, k, block):
        return [ref[k, rows(block), f * LANES : (f + 1) * LANES] for f in range(3)]

    def store(ref, k, block, values):
        for f in range(3):
            ref[k, rows(block), f * LANES : (f + 1) * LANES] = values[f]

    centre = lax.broadcasted_iota(jnp.int32, (8, LANES), 1)
    centre = (centre >= LANES // 4) & (centre < 3 * LANES // 4)

    def blocks(low, high):
        return range(low // 8, high // 8 + 1)

    def chebyshev(low, high):
        for k in range(1, TERMS):
            for block in blocks(low + k, high - k):
                new = operator(p_ref, k - 1, block)
                if k == 1:
                    new = [0.5 * value for value in new]
                else:
                    new = [a + b for a, b in zip(new, fields(p_ref, k - 2, block))]
                store(p_ref, k, block, new)

    def terms_at(row):
        return p_ref[:, PAD + row : PAD + row + 8, :]

    def wave(n, left, right):
        values = [terms_at(left)[:, :, f * LANES : (f + 1) * LANES].reshape(80, LANES) for f in range(3)]
        if right is not None:
            inside = jnp.concatenate([centre] * 10, axis=0)
            for f in range(3):
                other = terms_at(right)[:, :, f * LANES : (f + 1) * LANES].reshape(80, LANES)
                values[f] = jnp.where(inside, values[f], pltpu.roll(other, LANES // 2, 1))
        if EXTRA:
            values = values + [east(values[1]), east(values[2])]
        high, low = split(jnp.concatenate(values, axis=1))
        stacked = jnp.concatenate([high, low, high, jnp.zeros((16, SENT), bf16)], axis=0)
        waves = jnp.dot(forward_ref[...], stacked, preferred_element_type=f32)
        w_ref[:, 8 + 8 * n : 16 + 8 * n, :] = waves.reshape(SAMPLES, 8, SENT)

    def advect(s, n):
        def at(f, offset=0):
            return w_ref[s, 8 + 8 * n + offset : 16 + 8 * n + offset, f * LANES : (f + 1) * LANES]

        h, u, v = at(0), at(1), at(2)
        v_up, v_down = at(2, 1), at(2, -1)
        u_east, v_east = (at(3), at(4)) if EXTRA else (east(u), east(v))
        out_h = east(h * u) + (at(0, 1) * v_up - at(0, -1) * v_down)
        out_u = u * u_east + v * (at(1, 1) - at(1, -1))
        out_v = u * v_east + v * (v_up - v_down)
        return out_h, out_u, out_v

    def pulled(pair, n):
        one, two = advect(2 * pair, n), advect(2 * pair + 1, n)
        for f in range(3):
            high, low = split(jnp.concatenate([one[f], two[f]], axis=0))
            yh_ref[n, pair, :, f * LANES : (f + 1) * LANES] = high
            yl_ref[n, pair, :, f * LANES : (f + 1) * LANES] = low

    def weighted(n):
        both = jnp.dot(backh_ref[...], yh_ref[n].reshape(256, WIDE), preferred_element_type=f32)
        low = jnp.dot(backl_ref[...], yl_ref[n].reshape(256, WIDE), preferred_element_type=f32)
        return (both[0:80] + both[80:160] + low) * -0.5

    def put(total, row, first, last, turn):
        at = slice(PAD + row + first, PAD + row + last)
        mask = mask_ref[at, :]
        for k in range(TERMS):
            for f in range(3):
                value = total[8 * k : 8 * k + 8, f * LANES : (f + 1) * LANES]
                if turn:
                    value = pltpu.roll(value, LANES // 2, 1)
                value = value[first:last]
                z_ref[k, at, f * LANES : (f + 1) * LANES] = value * mask if f == 0 else value

    def mid(plan):
        count = len(plan)

        def finish(n):
            total = weighted(n)
            for row, first, last, turn in plan[n][2]:
                put(total, row, first, last, turn)

        if PIPELINED:
            wave(0, *plan[0][:2])
            for n in range(count):
                if n + 1 < count:
                    wave(n + 1, *plan[n + 1][:2])
                for pair in range(SAMPLES // 2):
                    pulled(pair, n)
                if n > 0:
                    finish(n - 1)
            finish(count - 1)
        else:
            for n in range(count):
                wave(n, *plan[n][:2])

            def pairs(pair, carry):
                for n in range(count):
                    pulled(pair, n)
                return carry

            lax.fori_loop(0, SAMPLES // 2, pairs, 0)
            for n in range(count):
                finish(n)

    def clenshaw(low, high):
        for k in range(DEG - 1, -1, -1):
            for block in blocks(low - k, high + k):
                new = operator(z_ref, k + 1, block)
                if k == 0:
                    new = [0.5 * value for value in new]
                new = [a + b for a, b in zip(new, fields(z_ref, k, block))]
                if k + 2 < TERMS:
                    new = [a + b for a, b in zip(new, fields(z_ref, k + 2, block))]
                store(z_ref, k, block, new)

    chebyshev(2, 101)
    mid(
        [(24 + 8 * n, None, [(24 + 8 * n, 1 if n == 0 else 0, 7 if n == 6 else 8, False)]) for n in range(7)]
        + [(10, 78, [(10, 1, 8, False), (78, 1, 8, True)]), (18, 86, [(18, 0, 7, False), (86, 0, 7, True)])]
    )
    clenshaw(19, 84)
    for block in range(2, 11):
        at = rows(block)
        t_ref[at, :] = z_ref[0, at, :]
        p_ref[0, at, :] = p_ref[0, at, :] + STEP * z_ref[0, at, :]
    chebyshev(19, 84)
    mid(
        [
            (24, 48, [(24, 0, 8, False), (48, 4, 8, True)]),
            (32, 56, [(32, 0, 8, False), (56, 0, 8, True)]),
            (40, 64, [(40, 0, 8, False), (64, 0, 8, True)]),
            (48, 72, [(48, 0, 4, False), (72, 0, 8, True)]),
        ]
    )
    clenshaw(36, 67)
    at = slice(PAD + BASE, PAD + BASE + TILE)
    tendency = 0.5 * (t_ref[at, :] + z_ref[0, at, :])
    lanes = lax.broadcasted_iota(jnp.int32, (TILE, LANES), 1)
    parts = [pltpu.roll(tendency[:, f * LANES : (f + 1) * LANES], (TILE * f - LEFT) % LANES, 1) for f in range(3)]
    out_ref[...] = jnp.where(lanes < TILE, parts[0], jnp.where(lanes < 2 * TILE, parts[1], parts[2]))


def vmem():
    return pl.BlockSpec(memory_space=pltpu.VMEM)


def smem():
    return pl.BlockSpec(memory_space=pltpu.SMEM)


def pack(row, times, weights, cor, state, depth):
    grid = pltpu.PrefetchScalarGridSpec(
        num_scalar_prefetch=1,
        grid=(1,),
        in_specs=[
            smem(), smem(), smem(), vmem(),
            pl.BlockSpec((8, NLON), lambda i, at: (lax.div(at[0], 8), 0)),
            vmem(),
        ],
        out_specs=vmem(),
        scratch_shapes=[pltpu.VMEM((8, LANES), f32)],
    )
    return pl.pallas_call(
        pack_kernel,
        out_shape=jax.ShapeDtypeStruct((2 * TILE * 4, LANES), f32),
        grid_spec=grid,
        name="pack",
    )(row, times, weights, cor, state, depth, jnp.asarray(series_table()))


def tile(place, own, near, far):
    return pl.pallas_call(
        tile_kernel,
        out_shape=jax.ShapeDtypeStruct((TILE, LANES), f32),
        in_specs=[smem()] + [vmem()] * 3,
        out_specs=vmem(),
        scratch_shapes=[
            pltpu.VMEM((TERMS + 1, ROWS, WIDE), f32),
            pltpu.VMEM((TERMS, ROWS, WIDE), f32),
            pltpu.VMEM((SAMPLES, W_ROWS, SENT), f32),
            pltpu.VMEM((BLOCKS, SAMPLES // 2, 16, WIDE), bf16),
            pltpu.VMEM((BLOCKS, SAMPLES // 2, 16, WIDE), bf16),
            pltpu.VMEM((ROWS, WIDE), f32),
            pltpu.VMEM((ROWS, LANES), f32),
            pltpu.VMEM((ROWS, LANES), f32),
            pltpu.VMEM((ROWS, LANES), f32),
            pltpu.VMEM((256, 256), bf16),
            pltpu.VMEM((160, 256), bf16),
            pltpu.VMEM((80, 256), bf16),
        ],
        compiler_params=pltpu.CompilerParams(vmem_limit_bytes=48 * 1024 * 1024),
        name="tile",
    )(place, own, near, far)


def unpack(columns, state):
    shape = jax.ShapeDtypeStruct((3, 8, LANES), f32)
    return pl.pallas_call(
        unpack_kernel,
        out_shape=(shape, shape),
        in_specs=[vmem(), vmem()],
        out_specs=(vmem(), vmem()),
        name="unpack",
    )(columns, state)


def per_device(ring, state_now, ocean_depth, coriolis, phase_times, phase_weights):
    state = state_now.reshape(3, 8, LANES)
    row = lax.axis_index("phase").astype(jnp.int32)
    core = lax.axis_index("core").astype(jnp.int32)
    lat = 2 * lax.axis_index("ring").astype(jnp.int32) + core
    message = pack(row[None], phase_times, phase_weights, coriolis, state, ocean_depth)
    own = lax.all_to_all(message, ("core", "phase"), 0, 0, tiled=True)
    devices = ("phase", "ring", "core")
    moves = [(at, at + 1, 0) for at in range(ring - 1)] + [(at + 1, at, 1) for at in range(ring - 1)]
    pairs = [((p * ring + a) * 2 + c, (p * ring + b) * 2 + c) for p in range(TILE) for a, b, c in moves]
    near = lax.dynamic_slice_in_dim(own, jnp.where(core == 0, 4 * (TILE - 2), 0), 4 * (TILE + 2), 0)
    near = lax.ppermute(near, devices, pairs)
    far = lax.dynamic_slice_in_dim(near, jnp.where(core == 0, 4 * TILE, 0), 8, 0)
    far = lax.ppermute(far, "core", [(0, 1), (1, 0)])
    columns = tile(lat[None], own, near, far)
    columns = lax.all_to_all(columns, "phase", 0, 0, tiled=True)
    state_next, tendency = unpack(columns, state)
    return state_next.reshape(state_now.shape), tendency.reshape(state_now.shape)


def solution(mesh):
    phase, lat = mesh.shape["phase"], mesh.shape["lat"]
    mesh = jax.sharding.Mesh(mesh.devices.reshape(phase, lat // 2, 2), ("phase", "ring", "core"))
    rows = P(None, ("ring", "core", "phase"), None)
    return jax.shard_map(
        functools.partial(per_device, lat // 2),
        mesh=mesh,
        in_specs=(rows, P(("ring", "core"), None), P(("ring", "core")), P("phase"), P("phase")),
        out_specs=(rows, rows),
        check_vma=False,
    )
```

```python
import functools
import math

import jax
import jax.numpy as jnp
import numpy as np
from jax import lax
from jax.experimental import pallas as pl
from jax.experimental.pallas import tpu as pltpu
from jax.sharding import PartitionSpec as P

DEG = 8
TERMS = DEG + 1
SERIES = 20
SCALE = 2.5
STEP = 0.5
NLON = 1024

TILE = 32
LANES = 128
LEFT = 48
BASE = 36
BLOCKS = 13
PAD = 8
ROWS = PAD + 8 * BLOCKS + PAD
WIDE = 3 * LANES
EXTRA = False
PIPELINED = True
SENT = 5 * LANES if EXTRA else WIDE
W_ROWS = 8 * 9 + 16
TILE_SHAPES = [(256, 128), (136, 128), (8, 128)]
SAMPLES = 32

f32 = jnp.float32
bf16 = jnp.bfloat16


def series_table():
    table = np.zeros((24, LANES), np.float32)
    for m in range(SERIES):
        for k in range(TERMS):
            table[m, k] = (-1.0) ** m / (math.factorial(m) * math.factorial(m + k))
    return table


def pack_kernel(row_ref, time_ref, weight_ref, cor_ref, state_ref, depth_ref, table_ref, out_ref, line_ref):
    row = row_ref[0]
    lane = lax.broadcasted_iota(jnp.int32, (1, LANES), 1)
    half = jnp.broadcast_to(time_ref[...] * 0.5, (1, LANES))
    square = half * half
    total = jnp.zeros((1, LANES), f32)
    power = jnp.ones((1, LANES), f32)
    for m in range(SERIES):
        total = total + table_ref[m : m + 1, :] * power
        power = power * square
    scale = jnp.ones((1, LANES), f32)
    for k in range(1, TERMS):
        scale = jnp.where((lane >= k) & (lane < TERMS), scale * half, scale)
    forward = total * scale
    forward = jnp.where(lane == 0, forward, 2.0 * forward)
    backward = jnp.where(lane % 2 == 0, forward, -forward) * jnp.broadcast_to(weight_ref[...], (1, LANES))
    cor = jnp.full((1, LANES), cor_ref[row], f32)
    lanes = lax.broadcasted_iota(jnp.int32, (8, LANES), 1)
    mine = lax.broadcasted_iota(jnp.int32, (8, LANES), 0) == lax.rem(row, 8)
    for q in range(8):
        depth = depth_ref[:, q * LANES : (q + 1) * LANES]
        line_ref[q : q + 1, :] = jnp.sum(jnp.where(mine, depth, 0.0), axis=0, keepdims=True)
    extras = (forward, backward, None, cor)
    for f in range(4):
        here = state_ref[f] if f < 3 else line_ref[...]
        after = pltpu.roll(here, 7, 0)
        before = pltpu.roll(here, 1, 0)
        for c in range(4):
            start = TILE * c - LEFT
            first, second = (before, here) if start < 0 else (here, after)
            shift = start % LANES
            window = jnp.where(
                lanes < LANES - shift,
                pltpu.roll(first, LANES - shift, 1),
                pltpu.roll(second, LANES - shift, 1),
            )
            if extras[f] is not None:
                window = jnp.where(lanes < TERMS, jnp.broadcast_to(extras[f], (8, LANES)), window)
            for core in range(2):
                out_ref[pl.ds(4 * (TILE * core + c) + f, 8, stride=16), :] = window


def unpack_kernel(in_ref, state_ref, next_ref, tendency_ref):
    lanes = lax.broadcasted_iota(jnp.int32, (8, LANES), 1)
    for f in range(3):
        line = jnp.zeros((8, LANES), f32)
        for c in range(4):
            piece = in_ref[pl.ds(c, 8, stride=4), :]
            shift = (TILE * (c - f)) % LANES
            if shift:
                piece = pltpu.roll(piece, shift, 1)
            line = jnp.where((lanes >= TILE * c) & (lanes < TILE * (c + 1)), piece, line)
        tendency_ref[f] = line
        next_ref[f] = state_ref[f] + STEP * line


def split(value):
    high = value.astype(bf16)
    return high, (value - high.astype(f32)).astype(bf16)


def tile_kernel(
    place_ref, own_ref, near_ref, far_ref, out_ref,
    p_ref, z_ref, w_ref, yh_ref, yl_ref, t_ref, depth_ref, cor_ref, mask_ref, forward_ref, backh_ref, backl_ref,
):
    lat = place_ref[0]
    core = lax.rem(lat, 2)

    def rows(block, offset=0, count=1):
        start = PAD + 8 * block + offset
        return slice(start, start + 8 * count)

    edge = jnp.zeros((3, PAD + 8, LANES), f32)
    for k in range(TERMS):
        p_ref[k, :, 0 : PAD + 8, :] = edge
        p_ref[k, :, ROWS - PAD - 8 : ROWS, :] = edge
        z_ref[k, :, PAD : PAD + 16, :] = edge
        z_ref[k, :, ROWS - PAD - 16 : ROWS - PAD, :] = edge
    p_ref[TERMS] = jnp.zeros((3, ROWS, LANES), f32)
    for s in range(SAMPLES):
        w_ref[s, :, 0:8, :] = edge[:, :8] if not EXTRA else jnp.zeros((5, 8, LANES), f32)
        w_ref[s, :, W_ROWS - 8 : W_ROWS, :] = edge[:, :8] if not EXTRA else jnp.zeros((5, 8, LANES), f32)
    for ref in (depth_ref, cor_ref):
        ref[0 : PAD + 8, :] = jnp.zeros((PAD + 8, LANES), f32)
        ref[ROWS - PAD - 8 : ROWS, :] = jnp.zeros((PAD + 8, LANES), f32)

    def place(ref, count, at):
        at = PAD + BASE + at
        h, u, v, depth, = [ref[pl.ds(f, count, stride=4), :] for f in range(4)]
        p_ref[0, 0, at : at + count, :] = h
        p_ref[0, 1, at : at + count, :] = u
        p_ref[0, 2, at : at + count, :] = v
        depth_ref[at : at + count, :] = depth * 0.4
        cor_ref[at : at + count, :] = jnp.broadcast_to(depth[:, 0:1] * 0.8, (count, LANES))

    @pl.when(core == 0)
    def _():
        place(own_ref, 2 * TILE, 0)
        place(near_ref, TILE + 2, -TILE - 2)
        place(far_ref, 2, 2 * TILE)

    @pl.when(core == 1)
    def _():
        place(own_ref, 2 * TILE, -TILE)
        place(near_ref, TILE + 2, TILE)
        place(far_ref, 2, -TILE - 2)

    at_row = lax.broadcasted_iota(jnp.int32, (ROWS, LANES), 0) + (TILE * lat - BASE - PAD)
    mask_ref[...] = jnp.where((at_row >= 0) & (at_row < 8 * TILE), 1.0, 0.0).astype(f32)

    term = lax.broadcasted_iota(jnp.int32, (LANES, 256), 0)
    column = lax.broadcasted_iota(jnp.int32, (LANES, 256), 1)
    group = column // 8
    high_at = (group == term) | (group - 10 == term)
    low_at = group - 20 == term
    pick_high = jnp.where(high_at & (term < TERMS), 1.0, 0.0).astype(bf16)
    pick_low = jnp.where(low_at & (term < TERMS), 1.0, 0.0).astype(bf16)
    same = lax.broadcasted_iota(jnp.int32, (256, 256), 0) % 8 == lax.broadcasted_iota(jnp.int32, (256, 256), 1) % 8

    def spread(block):
        value = own_ref[pl.ds(block, SAMPLES, stride=4), :]
        return split(jnp.broadcast_to(value[:, None, :], (SAMPLES, 8, LANES)).reshape(256, LANES))

    def picked(value, pick):
        return jnp.dot(value, pick, preferred_element_type=f32)

    high, low = spread(0)
    forward = picked(high, pick_high) + picked(low, pick_low)
    forward_ref[...] = jnp.where(same, forward, 0.0).astype(bf16)
    high, low = spread(1)
    pick = jnp.where((group == term) & (term < TERMS), 1.0, 0.0).astype(bf16)[:, :LANES]
    back_high = jnp.where(same[:, :LANES], picked(high, pick), 0.0).T
    back_low = jnp.where(same[:, :LANES], picked(low, pick), 0.0).T
    backh_ref[0:80, :] = back_high[0:80].astype(bf16)
    backh_ref[80:160, :] = back_low[0:80].astype(bf16)
    backl_ref[...] = back_high[0:80].astype(bf16)

    def east(value):
        return pltpu.roll(value, LANES - 1, 1) - pltpu.roll(value, 1, 1)

    def operator(ref, k, block):
        mid, up, down = rows(block), rows(block, 1), rows(block, -1)
        h, u, v = ref[k, 0, mid, :], ref[k, 1, mid, :], ref[k, 2, mid, :]
        mask, cor = mask_ref[mid, :], cor_ref[mid, :]
        flux = east(depth_ref[mid, :] * u) + (depth_ref[up, :] * ref[k, 2, up, :] - depth_ref[down, :] * ref[k, 2, down, :])
        out_h = -(mask * flux)
        out_u = cor * v - 0.4 * east(h)
        out_v = mask * (-0.4 * (ref[k, 0, up, :] - ref[k, 0, down, :])) - cor * u
        return out_h, out_u, out_v

    def fields(ref, k, block):
        return [ref[k, f, rows(block), :] for f in range(3)]

    def store(ref, k, block, values):
        for f in range(3):
            ref[k, f, rows(block), :] = values[f]

    centre = lax.broadcasted_iota(jnp.int32, (8, LANES), 1)
    centre = (centre >= LANES // 4) & (centre < 3 * LANES // 4)

    def blocks(low, high):
        return range(low // 8, high // 8 + 1)

    def chebyshev(low, high):
        for k in range(1, TERMS):
            for block in blocks(low + k, high - k):
                new = operator(p_ref, k - 1, block)
                if k == 1:
                    new = [0.5 * value for value in new]
                else:
                    new = [a + b for a, b in zip(new, fields(p_ref, k - 2, block))]
                store(p_ref, k, block, new)

    def terms_at(f, row):
        return p_ref[:, f, PAD + row : PAD + row + 8, :].reshape(80, LANES)

    def wave(n, left, right):
        values = [terms_at(f, left) for f in range(3)]
        if right is not None:
            inside = jnp.concatenate([centre] * 10, axis=0)
            for f in range(3):
                values[f] = jnp.where(inside, values[f], pltpu.roll(terms_at(f, right), LANES // 2, 1))
        if EXTRA:
            values = values + [east(values[1]), east(values[2])]
        high, low = split(jnp.concatenate(values, axis=1))
        stacked = jnp.concatenate([high, low, high, jnp.zeros((16, SENT), bf16)], axis=0)
        waves = jnp.dot(forward_ref[...], stacked, preferred_element_type=f32)
        for f in range(len(values)):
            w_ref[:, f, 8 + 8 * n : 16 + 8 * n, :] = waves[:, f * LANES : (f + 1) * LANES].reshape(SAMPLES, 8, LANES)

    def advect(s, n):
        def at(f, offset=0):
            return w_ref[s, f, 8 + 8 * n + offset : 16 + 8 * n + offset, :]

        h, u, v = at(0), at(1), at(2)
        v_up, v_down = at(2, 1), at(2, -1)
        u_east, v_east = (at(3), at(4)) if EXTRA else (east(u), east(v))
        out_h = east(h * u) + (at(0, 1) * v_up - at(0, -1) * v_down)
        out_u = u * u_east + v * (at(1, 1) - at(1, -1))
        out_v = u * v_east + v * (v_up - v_down)
        return out_h, out_u, out_v

    def pulled(pair, n):
        one, two = advect(2 * pair, n), advect(2 * pair + 1, n)
        for f in range(3):
            high, low = split(jnp.concatenate([one[f], two[f]], axis=0))
            yh_ref[n, pair, :, f * LANES : (f + 1) * LANES] = high
            yl_ref[n, pair, :, f * LANES : (f + 1) * LANES] = low

    def weighted(n):
        both = jnp.dot(backh_ref[...], yh_ref[n].reshape(256, WIDE), preferred_element_type=f32)
        low = jnp.dot(backl_ref[...], yl_ref[n].reshape(256, WIDE), preferred_element_type=f32)
        return (both[0:80] + both[80:160] + low) * -0.5

    def put(total, row, first, last, turn):
        at = slice(PAD + row + first, PAD + row + last)
        mask = mask_ref[at, :]
        for k in range(TERMS):
            for f in range(3):
                value = total[8 * k : 8 * k + 8, f * LANES : (f + 1) * LANES]
                if turn:
                    value = pltpu.roll(value, LANES // 2, 1)
                value = value[first:last]
                z_ref[k, f, at, :] = value * mask if f == 0 else value

    def mid(plan):
        count = len(plan)

        def finish(n):
            total = weighted(n)
            for row, first, last, turn in plan[n][2]:
                put(total, row, first, last, turn)

        if PIPELINED:
            wave(0, *plan[0][:2])
            for n in range(count):
                if n + 1 < count:
                    wave(n + 1, *plan[n + 1][:2])
                for pair in range(SAMPLES // 2):
                    pulled(pair, n)
                if n > 0:
                    finish(n - 1)
            finish(count - 1)
        else:
            for n in range(count):
                wave(n, *plan[n][:2])

            def pairs(pair, carry):
                for n in range(count):
                    pulled(pair, n)
                return carry

            lax.fori_loop(0, SAMPLES // 2, pairs, 0)
            for n in range(count):
                finish(n)

    def clenshaw(low, high):
        for k in range(DEG - 1, -1, -1):
            for block in blocks(low - k, high + k):
                new = operator(z_ref, k + 1, block)
                if k == 0:
                    new = [0.5 * value for value in new]
                new = [a + b for a, b in zip(new, fields(z_ref, k, block))]
                if k + 2 < TERMS:
                    new = [a + b for a, b in zip(new, fields(z_ref, k + 2, block))]
                store(z_ref, k, block, new)

    chebyshev(2, 101)
    mid(
        [(24 + 8 * n, None, [(24 + 8 * n, 1 if n == 0 else 0, 7 if n == 6 else 8, False)]) for n in range(7)]
        + [(10, 78, [(10, 1, 8, False), (78, 1, 8, True)]), (18, 86, [(18, 0, 7, False), (86, 0, 7, True)])]
    )
    clenshaw(19, 84)
    for block in range(2, 11):
        at = rows(block)
        t_ref[:, at, :] = z_ref[0, :, at, :]
        p_ref[0, :, at, :] = p_ref[0, :, at, :] + STEP * z_ref[0, :, at, :]
    chebyshev(19, 84)
    mid(
        [
            (24, 48, [(24, 0, 8, False), (48, 4, 8, True)]),
            (32, 56, [(32, 0, 8, False), (56, 0, 8, True)]),
            (40, 64, [(40, 0, 8, False), (64, 0, 8, True)]),
            (48, 72, [(48, 0, 4, False), (72, 0, 8, True)]),
        ]
    )
    clenshaw(36, 67)
    at = slice(PAD + BASE, PAD + BASE + TILE)
    tendency = 0.5 * (t_ref[:, at, :] + z_ref[0, :, at, :])
    lanes = lax.broadcasted_iota(jnp.int32, (TILE, LANES), 1)
    parts = [pltpu.roll(tendency[f], (TILE * f - LEFT) % LANES, 1) for f in range(3)]
    out_ref[...] = jnp.where(lanes < TILE, parts[0], jnp.where(lanes < 2 * TILE, parts[1], parts[2]))


def vmem():
    return pl.BlockSpec(memory_space=pltpu.VMEM)


def smem():
    return pl.BlockSpec(memory_space=pltpu.SMEM)


def pack(row, times, weights, cor, state, depth):
    grid = pltpu.PrefetchScalarGridSpec(
        num_scalar_prefetch=1,
        grid=(1,),
        in_specs=[
            vmem(), vmem(), smem(), vmem(),
            pl.BlockSpec((8, NLON), lambda i, at: (lax.div(at[0], 8), 0)),
            vmem(),
        ],
        out_specs=vmem(),
        scratch_shapes=[pltpu.VMEM((8, LANES), f32)],
    )
    return pl.pallas_call(
        pack_kernel,
        out_shape=jax.ShapeDtypeStruct((2 * TILE * 4, LANES), f32),
        grid_spec=grid,
        name="pack",
    )(row, times.reshape(1, 1), weights.reshape(1, 1), cor, state, depth, jnp.asarray(series_table()))


def tile(place, own, near, far):
    return pl.pallas_call(
        tile_kernel,
        out_shape=jax.ShapeDtypeStruct((TILE, LANES), f32),
        in_specs=[smem()] + [vmem()] * 3,
        out_specs=vmem(),
        scratch_shapes=[
            pltpu.VMEM((TERMS + 1, 3, ROWS, LANES), f32),
            pltpu.VMEM((TERMS, 3, ROWS, LANES), f32),
            pltpu.VMEM((SAMPLES, SENT // LANES, W_ROWS, LANES), f32),
            pltpu.VMEM((BLOCKS, SAMPLES // 2, 16, WIDE), bf16),
            pltpu.VMEM((BLOCKS, SAMPLES // 2, 16, WIDE), bf16),
            pltpu.VMEM((3, ROWS, LANES), f32),
            pltpu.VMEM((ROWS, LANES), f32),
            pltpu.VMEM((ROWS, LANES), f32),
            pltpu.VMEM((ROWS, LANES), f32),
            pltpu.VMEM((256, 256), bf16),
            pltpu.VMEM((160, 256), bf16),
            pltpu.VMEM((80, 256), bf16),
        ],
        compiler_params=pltpu.CompilerParams(vmem_limit_bytes=48 * 1024 * 1024),
        name="tile",
    )(place, own, near, far)


def unpack(columns, state):
    shape = jax.ShapeDtypeStruct((3, 8, LANES), f32)
    return pl.pallas_call(
        unpack_kernel,
        out_shape=(shape, shape),
        in_specs=[vmem(), vmem()],
        out_specs=(vmem(), vmem()),
        name="unpack",
    )(columns, state)


def per_device(ring, state_now, ocean_depth, coriolis, phase_times, phase_weights):
    state = state_now.reshape(3, 8, LANES)
    row = lax.axis_index("phase").astype(jnp.int32)
    core = lax.axis_index("core").astype(jnp.int32)
    lat = 2 * lax.axis_index("ring").astype(jnp.int32) + core
    message = pack(row[None], phase_times, phase_weights, coriolis, state, ocean_depth)
    own = lax.all_to_all(message, ("core", "phase"), 0, 0, tiled=True)
    devices = ("phase", "ring", "core")
    moves = [(at, at + 1, 0) for at in range(ring - 1)] + [(at + 1, at, 1) for at in range(ring - 1)]
    pairs = [((p * ring + a) * 2 + c, (p * ring + b) * 2 + c) for p in range(TILE) for a, b, c in moves]
    near = lax.dynamic_slice_in_dim(own, jnp.where(core == 0, 4 * (TILE - 2), 0), 4 * (TILE + 2), 0)
    near = lax.ppermute(near, devices, pairs)
    far = lax.dynamic_slice_in_dim(near, jnp.where(core == 0, 4 * TILE, 0), 8, 0)
    far = lax.ppermute(far, "core", [(0, 1), (1, 0)])
    columns = tile(lat[None], own, near, far)
    columns = lax.all_to_all(columns, "phase", 0, 0, tiled=True)
    state_next, tendency = unpack(columns, state)
    return state_next.reshape(state_now.shape), tendency.reshape(state_now.shape)


def solution(mesh):
    phase, lat = mesh.shape["phase"], mesh.shape["lat"]
    mesh = jax.sharding.Mesh(mesh.devices.reshape(phase, lat // 2, 2), ("phase", "ring", "core"))
    rows = P(None, ("ring", "core", "phase"), None)
    return jax.shard_map(
        functools.partial(per_device, lat // 2),
        mesh=mesh,
        in_specs=(rows, P(("ring", "core"), None), P(("ring", "core")), P("phase"), P("phase")),
        out_specs=(rows, rows),
        check_vma=False,
    )
```

```python
import functools
import math

import jax
import jax.numpy as jnp
import numpy as np
from jax import lax
from jax.experimental import pallas as pl
from jax.experimental.pallas import tpu as pltpu
from jax.sharding import PartitionSpec as P

DEG = 8
TERMS = DEG + 1
SERIES = 20
SCALE = 2.5
STEP = 0.5
NLON = 1024

TILE = 32
LANES = 128
LEFT = 48
BASE = 36
BLOCKS = 13
PAD = 8
ROWS = PAD + 8 * BLOCKS + PAD
WIDE = 3 * LANES
EXTRA = False
PIPELINED = True
SENT = 5 * LANES if EXTRA else WIDE
W_ROWS = 8 * 9 + 16
TILE_SHAPES = [(256, 128), (136, 128), (8, 128)]
SAMPLES = 32

f32 = jnp.float32
bf16 = jnp.bfloat16


def series_table():
    table = np.zeros((24, LANES), np.float32)
    for m in range(SERIES):
        for k in range(TERMS):
            table[m, k] = (-1.0) ** m / (math.factorial(m) * math.factorial(m + k))
    return table


def pack_kernel(row_ref, time_ref, weight_ref, cor_ref, state_ref, depth_ref, table_ref, out_ref, line_ref):
    row = row_ref[0]
    lane = lax.broadcasted_iota(jnp.int32, (1, LANES), 1)
    half = jnp.broadcast_to(time_ref[...] * 0.5, (1, LANES))
    square = half * half
    total = jnp.zeros((1, LANES), f32)
    power = jnp.ones((1, LANES), f32)
    for m in range(SERIES):
        total = total + table_ref[m : m + 1, :] * power
        power = power * square
    scale = jnp.ones((1, LANES), f32)
    for k in range(1, TERMS):
        scale = jnp.where((lane >= k) & (lane < TERMS), scale * half, scale)
    forward = total * scale
    forward = jnp.where(lane == 0, forward, 2.0 * forward)
    backward = jnp.where(lane % 2 == 0, forward, -forward) * jnp.broadcast_to(weight_ref[...], (1, LANES))
    cor = jnp.full((1, LANES), cor_ref[row], f32)
    lanes = lax.broadcasted_iota(jnp.int32, (8, LANES), 1)
    mine = lax.broadcasted_iota(jnp.int32, (8, LANES), 0) == lax.rem(row, 8)
    for q in range(8):
        depth = depth_ref[:, q * LANES : (q + 1) * LANES]
        line_ref[q : q + 1, :] = jnp.sum(jnp.where(mine, depth, 0.0), axis=0, keepdims=True)
    extras = (forward, backward, None, cor)
    for f in range(4):
        here = state_ref[f] if f < 3 else line_ref[...]
        after = pltpu.roll(here, 7, 0)
        before = pltpu.roll(here, 1, 0)
        for c in range(4):
            start = TILE * c - LEFT
            first, second = (before, here) if start < 0 else (here, after)
            shift = start % LANES
            window = jnp.where(
                lanes < LANES - shift,
                pltpu.roll(first, LANES - shift, 1),
                pltpu.roll(second, LANES - shift, 1),
            )
            if extras[f] is not None:
                window = jnp.where(lanes < TERMS, jnp.broadcast_to(extras[f], (8, LANES)), window)
            for core in range(2):
                out_ref[pl.ds(4 * (TILE * core + c) + f, 8, stride=16), :] = window


def unpack_kernel(in_ref, state_ref, next_ref, tendency_ref):
    lanes = lax.broadcasted_iota(jnp.int32, (8, LANES), 1)
    for f in range(3):
        line = jnp.zeros((8, LANES), f32)
        for c in range(4):
            piece = in_ref[pl.ds(c, 8, stride=4), :]
            shift = (TILE * (c - f)) % LANES
            if shift:
                piece = pltpu.roll(piece, shift, 1)
            line = jnp.where((lanes >= TILE * c) & (lanes < TILE * (c + 1)), piece, line)
        tendency_ref[f] = line
        next_ref[f] = state_ref[f] + STEP * line


def split(value):
    high = value.astype(bf16)
    return high, (value - high.astype(f32)).astype(bf16)


def tile_kernel(
    place_ref, own_ref, near_ref, far_ref, out_ref,
    p_ref, z_ref, w_ref, yh_ref, yl_ref, t_ref, depth_ref, cor_ref, mask_ref, forward_ref, backh_ref, backl_ref,
):
    lat = place_ref[0]
    core = lax.rem(lat, 2)

    def rows(block, offset=0, count=1):
        start = PAD + 8 * block + offset
        return slice(start, start + 8 * count)

    edge = jnp.zeros((3, PAD + 8, LANES), f32)
    for k in range(TERMS):
        p_ref[k, :, 0 : PAD + 8, :] = edge
        p_ref[k, :, ROWS - PAD - 8 : ROWS, :] = edge
        z_ref[k, :, PAD : PAD + 16, :] = edge
        z_ref[k, :, ROWS - PAD - 16 : ROWS - PAD, :] = edge
    p_ref[TERMS] = jnp.zeros((3, ROWS, LANES), f32)
    for s in range(SAMPLES):
        w_ref[s, :, 0:8, :] = edge[:, :8] if not EXTRA else jnp.zeros((5, 8, LANES), f32)
        w_ref[s, :, W_ROWS - 8 : W_ROWS, :] = edge[:, :8] if not EXTRA else jnp.zeros((5, 8, LANES), f32)
    for ref in (depth_ref, cor_ref):
        ref[0 : PAD + 8, :] = jnp.zeros((PAD + 8, LANES), f32)
        ref[ROWS - PAD - 8 : ROWS, :] = jnp.zeros((PAD + 8, LANES), f32)

    def place(ref, count, at):
        at = PAD + BASE + at
        h, u, v, depth, = [ref[pl.ds(f, count, stride=4), :] for f in range(4)]
        p_ref[0, 0, at : at + count, :] = h
        p_ref[0, 1, at : at + count, :] = u
        p_ref[0, 2, at : at + count, :] = v
        depth_ref[at : at + count, :] = depth * 0.4
        cor_ref[at : at + count, :] = jnp.broadcast_to(depth[:, 0:1] * 0.8, (count, LANES))

    @pl.when(core == 0)
    def _():
        place(own_ref, 2 * TILE, 0)
        place(near_ref, TILE + 2, -TILE - 2)
        place(far_ref, 2, 2 * TILE)

    @pl.when(core == 1)
    def _():
        place(own_ref, 2 * TILE, -TILE)
        place(near_ref, TILE + 2, TILE)
        place(far_ref, 2, -TILE - 2)

    at_row = lax.broadcasted_iota(jnp.int32, (ROWS, LANES), 0) + (TILE * lat - BASE - PAD)
    mask_ref[...] = jnp.where((at_row >= 0) & (at_row < 8 * TILE), 1.0, 0.0).astype(f32)

    term = lax.broadcasted_iota(jnp.int32, (LANES, 256), 0)
    column = lax.broadcasted_iota(jnp.int32, (LANES, 256), 1)
    group = column // 8
    high_at = (group == term) | (group - 10 == term)
    low_at = group - 20 == term
    pick_high = jnp.where(high_at & (term < TERMS), 1.0, 0.0).astype(bf16)
    pick_low = jnp.where(low_at & (term < TERMS), 1.0, 0.0).astype(bf16)
    same = lax.broadcasted_iota(jnp.int32, (256, 256), 0) % 8 == lax.broadcasted_iota(jnp.int32, (256, 256), 1) % 8

    def spread(block):
        value = own_ref[pl.ds(block, SAMPLES, stride=4), :]
        return split(jnp.broadcast_to(value[:, None, :], (SAMPLES, 8, LANES)).reshape(256, LANES))

    def picked(value, pick):
        return jnp.dot(value, pick, preferred_element_type=f32)

    high, low = spread(0)
    forward = picked(high, pick_high) + picked(low, pick_low)
    forward_ref[...] = jnp.where(same, forward, 0.0).astype(bf16)
    high, low = spread(1)
    pick = jnp.where((group == term) & (term < TERMS), 1.0, 0.0).astype(bf16)[:, :LANES]
    back_high = jnp.where(same[:, :LANES], picked(high, pick), 0.0).T
    back_low = jnp.where(same[:, :LANES], picked(low, pick), 0.0).T
    backh_ref[0:80, :] = back_high[0:80].astype(bf16)
    backh_ref[80:160, :] = back_low[0:80].astype(bf16)
    backl_ref[...] = back_high[0:80].astype(bf16)

    def east(value):
        return pltpu.roll(value, LANES - 1, 1) - pltpu.roll(value, 1, 1)

    def operator(ref, k, block):
        mid, up, down = rows(block), rows(block, 1), rows(block, -1)
        h, u, v = ref[k, 0, mid, :], ref[k, 1, mid, :], ref[k, 2, mid, :]
        mask, cor = mask_ref[mid, :], cor_ref[mid, :]
        flux = east(depth_ref[mid, :] * u) + (depth_ref[up, :] * ref[k, 2, up, :] - depth_ref[down, :] * ref[k, 2, down, :])
        out_h = -(mask * flux)
        out_u = cor * v - 0.4 * east(h)
        out_v = mask * (-0.4 * (ref[k, 0, up, :] - ref[k, 0, down, :])) - cor * u
        return out_h, out_u, out_v

    def fields(ref, k, block):
        return [ref[k, f, rows(block), :] for f in range(3)]

    def store(ref, k, block, values):
        for f in range(3):
            ref[k, f, rows(block), :] = values[f]

    centre = lax.broadcasted_iota(jnp.int32, (8, LANES), 1)
    centre = (centre >= LANES // 4) & (centre < 3 * LANES // 4)

    def blocks(low, high):
        return range(low // 8, high // 8 + 1)

    def chebyshev(low, high):
        for k in range(1, TERMS):
            for block in blocks(low + k, high - k):
                new = operator(p_ref, k - 1, block)
                if k == 1:
                    new = [0.5 * value for value in new]
                else:
                    new = [a + b for a, b in zip(new, fields(p_ref, k - 2, block))]
                store(p_ref, k, block, new)

    def terms_at(f, row):
        return p_ref[:, f, PAD + row : PAD + row + 8, :].reshape(80, LANES)

    def wave(n, left, right):
        values = [terms_at(f, left) for f in range(3)]
        if right is not None:
            inside = jnp.concatenate([centre] * 10, axis=0)
            for f in range(3):
                values[f] = jnp.where(inside, values[f], pltpu.roll(terms_at(f, right), LANES // 2, 1))
        if EXTRA:
            values = values + [east(values[1]), east(values[2])]
        high, low = split(jnp.concatenate(values, axis=1))
        stacked = jnp.concatenate([high, low, high, jnp.zeros((16, SENT), bf16)], axis=0)
        waves = jnp.dot(forward_ref[...], stacked, preferred_element_type=f32)
        for f in range(len(values)):
            w_ref[:, f, 8 + 8 * n : 16 + 8 * n, :] = waves[:, f * LANES : (f + 1) * LANES].reshape(SAMPLES, 8, LANES)

    def advect(s, n):
        def at(f, offset=0):
            return w_ref[s, f, 8 + 8 * n + offset : 16 + 8 * n + offset, :]

        h, u, v = at(0), at(1), at(2)
        v_up, v_down = at(2, 1), at(2, -1)
        u_east, v_east = (at(3), at(4)) if EXTRA else (east(u), east(v))
        out_h = east(h * u) + (at(0, 1) * v_up - at(0, -1) * v_down)
        out_u = u * u_east + v * (at(1, 1) - at(1, -1))
        out_v = u * v_east + v * (v_up - v_down)
        return out_h, out_u, out_v

    def pulled(pair, n):
        one, two = advect(2 * pair, n), advect(2 * pair + 1, n)
        for f in range(3):
            high, low = split(jnp.concatenate([one[f], two[f]], axis=0))
            yh_ref[n, pair, :, f * LANES : (f + 1) * LANES] = high
            yl_ref[n, pair, :, f * LANES : (f + 1) * LANES] = low

    def weighted(n):
        both = jnp.dot(backh_ref[...], yh_ref[n].reshape(256, WIDE), preferred_element_type=f32)
        low = jnp.dot(backl_ref[...], yl_ref[n].reshape(256, WIDE), preferred_element_type=f32)
        return (both[0:80] + both[80:160] + low) * -0.5

    def put(total, row, first, last, turn):
        at = slice(PAD + row + first, PAD + row + last)
        mask = mask_ref[at, :]
        for k in range(TERMS):
            for f in range(3):
                value = total[8 * k : 8 * k + 8, f * LANES : (f + 1) * LANES]
                if turn:
                    value = pltpu.roll(value, LANES // 2, 1)
                value = value[first:last]
                z_ref[k, f, at, :] = value * mask if f == 0 else value

    def mid(plan):
        count = len(plan)

        def finish(n):
            total = weighted(n)
            for row, first, last, turn in plan[n][2]:
                put(total, row, first, last, turn)

        if PIPELINED:
            wave(0, *plan[0][:2])
            for n in range(count):
                if n + 1 < count:
                    wave(n + 1, *plan[n + 1][:2])
                for pair in range(SAMPLES // 2):
                    pulled(pair, n)
                if n > 0:
                    finish(n - 1)
            finish(count - 1)
        else:
            for n in range(count):
                wave(n, *plan[n][:2])

            def pairs(pair, carry):
                for n in range(count):
                    pulled(pair, n)
                return carry

            lax.fori_loop(0, SAMPLES // 2, pairs, 0)
            for n in range(count):
                finish(n)

    def clenshaw(low, high):
        for k in range(DEG - 1, -1, -1):
            for block in blocks(low - k, high + k):
                new = operator(z_ref, k + 1, block)
                if k == 0:
                    new = [0.5 * value for value in new]
                new = [a + b for a, b in zip(new, fields(z_ref, k, block))]
                if k + 2 < TERMS:
                    new = [a + b for a, b in zip(new, fields(z_ref, k + 2, block))]
                store(z_ref, k, block, new)

    chebyshev(2, 101)
    mid(
        [(24 + 8 * n, None, [(24 + 8 * n, 1 if n == 0 else 0, 7 if n == 6 else 8, False)]) for n in range(7)]
        + [(10, 78, [(10, 1, 8, False), (78, 1, 8, True)]), (18, 86, [(18, 0, 7, False), (86, 0, 7, True)])]
    )
    clenshaw(19, 84)
    for block in range(2, 11):
        at = rows(block)
        t_ref[:, at, :] = z_ref[0, :, at, :]
        p_ref[0, :, at, :] = p_ref[0, :, at, :] + STEP * z_ref[0, :, at, :]
    chebyshev(19, 84)
    mid(
        [
            (24, 48, [(24, 0, 8, False), (48, 4, 8, True)]),
            (32, 56, [(32, 0, 8, False), (56, 0, 8, True)]),
            (40, 64, [(40, 0, 8, False), (64, 0, 8, True)]),
            (48, 72, [(48, 0, 4, False), (72, 0, 8, True)]),
        ]
    )
    clenshaw(36, 67)
    at = slice(PAD + BASE, PAD + BASE + TILE)
    tendency = 0.5 * (t_ref[:, at, :] + z_ref[0, :, at, :])
    lanes = lax.broadcasted_iota(jnp.int32, (TILE, LANES), 1)
    parts = [pltpu.roll(tendency[f], (TILE * f - LEFT) % LANES, 1) for f in range(3)]
    out_ref[...] = jnp.where(lanes < TILE, parts[0], jnp.where(lanes < 2 * TILE, parts[1], parts[2]))


def vmem():
    return pl.BlockSpec(memory_space=pltpu.VMEM)


def smem():
    return pl.BlockSpec(memory_space=pltpu.SMEM)


def pack(row, times, weights, cor, state, depth):
    grid = pltpu.PrefetchScalarGridSpec(
        num_scalar_prefetch=1,
        grid=(1,),
        in_specs=[
            vmem(), vmem(), smem(), vmem(),
            pl.BlockSpec((8, NLON), lambda i, at: (lax.div(at[0], 8), 0)),
            vmem(),
        ],
        out_specs=vmem(),
        scratch_shapes=[pltpu.VMEM((8, LANES), f32)],
    )
    return pl.pallas_call(
        pack_kernel,
        out_shape=jax.ShapeDtypeStruct((2 * TILE * 4, LANES), f32),
        grid_spec=grid,
        name="pack",
    )(row, times.reshape(1, 1), weights.reshape(1, 1), cor, state, depth, jnp.asarray(series_table()))


def tile(place, own, near, far):
    return pl.pallas_call(
        tile_kernel,
        out_shape=jax.ShapeDtypeStruct((TILE, LANES), f32),
        in_specs=[smem()] + [vmem()] * 3,
        out_specs=vmem(),
        scratch_shapes=[
            pltpu.VMEM((TERMS + 1, 3, ROWS, LANES), f32),
            pltpu.VMEM((TERMS, 3, ROWS, LANES), f32),
            pltpu.VMEM((SAMPLES, SENT // LANES, W_ROWS, LANES), f32),
            pltpu.VMEM((BLOCKS, SAMPLES // 2, 16, WIDE), bf16),
            pltpu.VMEM((BLOCKS, SAMPLES // 2, 16, WIDE), bf16),
            pltpu.VMEM((3, ROWS, LANES), f32),
            pltpu.VMEM((ROWS, LANES), f32),
            pltpu.VMEM((ROWS, LANES), f32),
            pltpu.VMEM((ROWS, LANES), f32),
            pltpu.VMEM((256, 256), bf16),
            pltpu.VMEM((160, 256), bf16),
            pltpu.VMEM((80, 256), bf16),
        ],
        compiler_params=pltpu.CompilerParams(vmem_limit_bytes=48 * 1024 * 1024),
        name="tile",
    )(place, own, near, far)


def unpack(columns, state):
    shape = jax.ShapeDtypeStruct((3, 8, LANES), f32)
    return pl.pallas_call(
        unpack_kernel,
        out_shape=(shape, shape),
        in_specs=[vmem(), vmem()],
        out_specs=(vmem(), vmem()),
        name="unpack",
    )(columns, state)


def per_device(ring, state_now, ocean_depth, coriolis, phase_times, phase_weights):
    state = state_now.reshape(3, 8, LANES)
    row = lax.axis_index("phase").astype(jnp.int32)
    core = lax.axis_index("core").astype(jnp.int32)
    lat = 2 * lax.axis_index("ring").astype(jnp.int32) + core
    message = pack(row[None], phase_times, phase_weights, coriolis, state, ocean_depth)
    near_at = jnp.where(core == 0, 4 * (TILE - 2), 0).astype(jnp.uint32)
    far_at = jnp.where(core == 0, 4 * TILE, 0).astype(jnp.uint32)
    message, near_at, far_at, lat = lax.optimization_barrier((message, near_at, far_at, lat))
    own = lax.all_to_all(message, ("core", "phase"), 0, 0, tiled=True)
    devices = ("phase", "ring", "core")
    moves = [(at, at + 1, 0) for at in range(ring - 1)] + [(at + 1, at, 1) for at in range(ring - 1)]
    pairs = [((p * ring + a) * 2 + c, (p * ring + b) * 2 + c) for p in range(TILE) for a, b, c in moves]
    near = lax.dynamic_slice_in_dim(own, near_at, 4 * (TILE + 2), 0)
    near = lax.ppermute(near, devices, pairs)
    far = lax.dynamic_slice_in_dim(near, far_at, 8, 0)
    far = lax.ppermute(far, "core", [(0, 1), (1, 0)])
    columns = tile(lat[None], own, near, far)
    columns = lax.all_to_all(columns, "phase", 0, 0, tiled=True)
    state_next, tendency = unpack(columns, state)
    return state_next.reshape(state_now.shape), tendency.reshape(state_now.shape)


def solution(mesh):
    phase, lat = mesh.shape["phase"], mesh.shape["lat"]
    mesh = jax.sharding.Mesh(mesh.devices.reshape(phase, lat // 2, 2), ("phase", "ring", "core"))
    rows = P(None, ("ring", "core", "phase"), None)
    return jax.shard_map(
        functools.partial(per_device, lat // 2),
        mesh=mesh,
        in_specs=(rows, P(("ring", "core"), None), P(("ring", "core")), P("phase"), P("phase")),
        out_specs=(rows, rows),
        check_vma=False,
    )
```

```python
import functools
import math

import jax
import jax.numpy as jnp
import numpy as np
from jax import lax
from jax.experimental import pallas as pl
from jax.experimental.pallas import tpu as pltpu
from jax.sharding import PartitionSpec as P

DEG = 8
TERMS = DEG + 1
SERIES = 20
SCALE = 2.5
STEP = 0.5
NLON = 1024

TILE = 32
LANES = 128
LEFT = 48
BASE = 36
BLOCKS = 13
PAD = 8
ROWS = PAD + 8 * BLOCKS + PAD
WIDE = 3 * LANES
EXTRA = False
PIPELINED = True
SENT = 5 * LANES if EXTRA else WIDE
W_ROWS = 8 * 9 + 16
TILE_SHAPES = [(256, 128), (136, 128), (8, 128)]
SAMPLES = 32

f32 = jnp.float32
bf16 = jnp.bfloat16


def series_table():
    table = np.zeros((24, LANES), np.float32)
    for m in range(SERIES):
        for k in range(TERMS):
            table[m, k] = (-1.0) ** m / (math.factorial(m) * math.factorial(m + k))
    return table


def pack_kernel(row_ref, time_ref, weight_ref, cor_ref, state_ref, depth_ref, table_ref, out_ref, line_ref):
    row = row_ref[0]
    lane = lax.broadcasted_iota(jnp.int32, (1, LANES), 1)
    half = jnp.broadcast_to(time_ref[...] * 0.5, (1, LANES))
    square = half * half
    total = jnp.zeros((1, LANES), f32)
    power = jnp.ones((1, LANES), f32)
    for m in range(SERIES):
        total = total + table_ref[m : m + 1, :] * power
        power = power * square
    scale = jnp.ones((1, LANES), f32)
    for k in range(1, TERMS):
        scale = jnp.where((lane >= k) & (lane < TERMS), scale * half, scale)
    forward = total * scale
    forward = jnp.where(lane == 0, forward, 2.0 * forward)
    backward = jnp.where(lane % 2 == 0, forward, -forward) * jnp.broadcast_to(weight_ref[...], (1, LANES))
    cor = jnp.full((1, LANES), cor_ref[row], f32)
    lanes = lax.broadcasted_iota(jnp.int32, (8, LANES), 1)
    mine = lax.broadcasted_iota(jnp.int32, (8, LANES), 0) == lax.rem(row, 8)
    for q in range(8):
        depth = depth_ref[:, q * LANES : (q + 1) * LANES]
        line_ref[q : q + 1, :] = jnp.sum(jnp.where(mine, depth, 0.0), axis=0, keepdims=True)
    extras = (forward, backward, None, cor)
    for f in range(4):
        here = state_ref[f] if f < 3 else line_ref[...]
        after = pltpu.roll(here, 7, 0)
        before = pltpu.roll(here, 1, 0)
        for c in range(4):
            start = TILE * c - LEFT
            first, second = (before, here) if start < 0 else (here, after)
            shift = start % LANES
            window = jnp.where(
                lanes < LANES - shift,
                pltpu.roll(first, LANES - shift, 1),
                pltpu.roll(second, LANES - shift, 1),
            )
            if extras[f] is not None:
                window = jnp.where(lanes < TERMS, jnp.broadcast_to(extras[f], (8, LANES)), window)
            for core in range(2):
                out_ref[pl.ds(4 * (TILE * core + c) + f, 8, stride=16), :] = window


def unpack_kernel(in_ref, state_ref, next_ref, tendency_ref):
    lanes = lax.broadcasted_iota(jnp.int32, (8, LANES), 1)
    for f in range(3):
        line = jnp.zeros((8, LANES), f32)
        for c in range(4):
            piece = in_ref[pl.ds(c, 8, stride=4), :]
            shift = (TILE * (c - f)) % LANES
            if shift:
                piece = pltpu.roll(piece, shift, 1)
            line = jnp.where((lanes >= TILE * c) & (lanes < TILE * (c + 1)), piece, line)
        tendency_ref[f] = line
        next_ref[f] = state_ref[f] + STEP * line


def split(value):
    high = value.astype(bf16)
    return high, (value - high.astype(f32)).astype(bf16)


def tile_kernel(
    place_ref, own_ref, near_ref, far_ref, out_ref,
    p_ref, z_ref, w_ref, yh_ref, yl_ref, t_ref, depth_ref, cor_ref, mask_ref, forward_ref, back_ref,
):
    lat = place_ref[0]
    core = lax.rem(lat, 2)

    def rows(block, offset=0, count=1):
        start = PAD + 8 * block + offset
        return slice(start, start + 8 * count)

    edge = jnp.zeros((3, PAD + 8, LANES), f32)
    for k in range(TERMS):
        p_ref[k, :, 0 : PAD + 8, :] = edge
        p_ref[k, :, ROWS - PAD - 8 : ROWS, :] = edge
        z_ref[k, :, PAD : PAD + 16, :] = edge
        z_ref[k, :, ROWS - PAD - 16 : ROWS - PAD, :] = edge
    p_ref[TERMS] = jnp.zeros((3, ROWS, LANES), f32)
    for s in range(SAMPLES):
        w_ref[s, :, 0:8, :] = edge[:, :8] if not EXTRA else jnp.zeros((5, 8, LANES), f32)
        w_ref[s, :, W_ROWS - 8 : W_ROWS, :] = edge[:, :8] if not EXTRA else jnp.zeros((5, 8, LANES), f32)
    for ref in (depth_ref, cor_ref):
        ref[0 : PAD + 8, :] = jnp.zeros((PAD + 8, LANES), f32)
        ref[ROWS - PAD - 8 : ROWS, :] = jnp.zeros((PAD + 8, LANES), f32)

    def place(ref, count, at):
        at = PAD + BASE + at
        h, u, v, depth, = [ref[pl.ds(f, count, stride=4), :] for f in range(4)]
        p_ref[0, 0, at : at + count, :] = h
        p_ref[0, 1, at : at + count, :] = u
        p_ref[0, 2, at : at + count, :] = v
        depth_ref[at : at + count, :] = depth * 0.4
        cor_ref[at : at + count, :] = jnp.broadcast_to(depth[:, 0:1] * 0.8, (count, LANES))

    @pl.when(core == 0)
    def _():
        place(own_ref, 2 * TILE, 0)
        place(near_ref, TILE + 2, -TILE - 2)
        place(far_ref, 2, 2 * TILE)

    @pl.when(core == 1)
    def _():
        place(own_ref, 2 * TILE, -TILE)
        place(near_ref, TILE + 2, TILE)
        place(far_ref, 2, -TILE - 2)

    at_row = lax.broadcasted_iota(jnp.int32, (ROWS, LANES), 0) + (TILE * lat - BASE - PAD)
    mask_ref[...] = jnp.where((at_row >= 0) & (at_row < 8 * TILE), 1.0, 0.0).astype(f32)

    term = lax.broadcasted_iota(jnp.int32, (LANES, 256), 0)
    column = lax.broadcasted_iota(jnp.int32, (LANES, 256), 1)
    group = column // 8
    high_at = (group == term) | (group - 10 == term)
    low_at = group - 20 == term
    pick_high = jnp.where(high_at & (term < TERMS), 1.0, 0.0).astype(bf16)
    pick_low = jnp.where(low_at & (term < TERMS), 1.0, 0.0).astype(bf16)
    same = lax.broadcasted_iota(jnp.int32, (256, 256), 0) % 8 == lax.broadcasted_iota(jnp.int32, (256, 256), 1) % 8

    def spread(block):
        value = own_ref[pl.ds(block, SAMPLES, stride=4), :]
        return split(jnp.broadcast_to(value[:, None, :], (SAMPLES, 8, LANES)).reshape(256, LANES))

    def picked(value, pick):
        return jnp.dot(value, pick, preferred_element_type=f32)

    high, low = spread(0)
    forward = picked(high, pick_high) + picked(low, pick_low)
    forward_ref[...] = jnp.where(same, forward, 0.0).astype(bf16)
    high, low = spread(1)
    line = lax.broadcasted_iota(jnp.int32, (80, LANES), 0) // 8
    term = lax.broadcasted_iota(jnp.int32, (80, LANES), 1)
    pick = jnp.where((line == term) & (term < TERMS), -0.5, 0.0).astype(bf16)

    def turned(value):
        value = lax.dot_general(pick, value, (((1,), (1,)), ((), ())), preferred_element_type=f32)
        return jnp.where(same[:80], value, 0.0).astype(bf16)

    back_high = turned(high)
    back_ref[:, 0:256] = back_high
    back_ref[:, 256:512] = turned(low)
    back_ref[:, 512:768] = back_high

    def east(value):
        return pltpu.roll(value, LANES - 1, 1) - pltpu.roll(value, 1, 1)

    def operator(ref, k, block):
        mid, up, down = rows(block), rows(block, 1), rows(block, -1)
        h, u, v = ref[k, 0, mid, :], ref[k, 1, mid, :], ref[k, 2, mid, :]
        mask, cor = mask_ref[mid, :], cor_ref[mid, :]
        flux = east(depth_ref[mid, :] * u) + (depth_ref[up, :] * ref[k, 2, up, :] - depth_ref[down, :] * ref[k, 2, down, :])
        out_h = -(mask * flux)
        out_u = cor * v - 0.4 * east(h)
        out_v = mask * (-0.4 * (ref[k, 0, up, :] - ref[k, 0, down, :])) - cor * u
        return out_h, out_u, out_v

    def fields(ref, k, block):
        return [ref[k, f, rows(block), :] for f in range(3)]

    def store(ref, k, block, values):
        for f in range(3):
            ref[k, f, rows(block), :] = values[f]

    centre = lax.broadcasted_iota(jnp.int32, (8, LANES), 1)
    centre = (centre >= LANES // 4) & (centre < 3 * LANES // 4)

    def blocks(low, high):
        return range(low // 8, high // 8 + 1)

    def chebyshev(low, high):
        for k in range(1, TERMS):
            for block in blocks(low + k, high - k):
                new = operator(p_ref, k - 1, block)
                if k == 1:
                    new = [0.5 * value for value in new]
                else:
                    new = [a + b for a, b in zip(new, fields(p_ref, k - 2, block))]
                store(p_ref, k, block, new)

    def terms_at(f, row):
        return p_ref[:, f, PAD + row : PAD + row + 8, :].reshape(80, LANES)

    def wave(n, left, right):
        values = [terms_at(f, left) for f in range(3)]
        if right is not None:
            inside = jnp.concatenate([centre] * 10, axis=0)
            for f in range(3):
                values[f] = jnp.where(inside, values[f], pltpu.roll(terms_at(f, right), LANES // 2, 1))
        if EXTRA:
            values = values + [east(values[1]), east(values[2])]
        high, low = split(jnp.concatenate(values, axis=1))
        stacked = jnp.concatenate([high, low, high, jnp.zeros((16, SENT), bf16)], axis=0)
        waves = jnp.dot(forward_ref[...], stacked, preferred_element_type=f32)
        for f in range(len(values)):
            w_ref[:, f, 8 + 8 * n : 16 + 8 * n, :] = waves[:, f * LANES : (f + 1) * LANES].reshape(SAMPLES, 8, LANES)

    def advect(s, n):
        def at(f, offset=0):
            return w_ref[s, f, 8 + 8 * n + offset : 16 + 8 * n + offset, :]

        h, u, v = at(0), at(1), at(2)
        v_up, v_down = at(2, 1), at(2, -1)
        u_east, v_east = (at(3), at(4)) if EXTRA else (east(u), east(v))
        out_h = east(h * u) + (at(0, 1) * v_up - at(0, -1) * v_down)
        out_u = u * u_east + v * (at(1, 1) - at(1, -1))
        out_v = u * v_east + v * (v_up - v_down)
        return out_h, out_u, out_v

    def pulled(pair, n):
        one, two = advect(2 * pair, n), advect(2 * pair + 1, n)
        for f in range(3):
            high, low = split(jnp.concatenate([one[f], two[f]], axis=0))
            yh_ref[n, pair, :, f * LANES : (f + 1) * LANES] = high
            yl_ref[n, pair, :, f * LANES : (f + 1) * LANES] = low

    def weighted(n):
        high, low = yh_ref[n].reshape(256, WIDE), yl_ref[n].reshape(256, WIDE)
        return jnp.dot(back_ref[...], jnp.concatenate([high, high, low], axis=0), preferred_element_type=f32)

    def put(total, row, first, last, turn):
        at = slice(PAD + row + first, PAD + row + last)
        mask = mask_ref[at, :]
        for k in range(TERMS):
            for f in range(3):
                value = total[8 * k : 8 * k + 8, f * LANES : (f + 1) * LANES]
                if turn:
                    value = pltpu.roll(value, LANES // 2, 1)
                value = value[first:last]
                z_ref[k, f, at, :] = value * mask if f == 0 else value

    def mid(plan):
        count = len(plan)

        def finish(n):
            total = weighted(n)
            for row, first, last, turn in plan[n][2]:
                put(total, row, first, last, turn)

        if PIPELINED:
            wave(0, *plan[0][:2])
            for n in range(count):
                if n + 1 < count:
                    wave(n + 1, *plan[n + 1][:2])
                for pair in range(SAMPLES // 2):
                    pulled(pair, n)
                if n > 0:
                    finish(n - 1)
            finish(count - 1)
        else:
            for n in range(count):
                wave(n, *plan[n][:2])

            def pairs(pair, carry):
                for n in range(count):
                    pulled(pair, n)
                return carry

            lax.fori_loop(0, SAMPLES // 2, pairs, 0)
            for n in range(count):
                finish(n)

    def clenshaw(low, high):
        for k in range(DEG - 1, -1, -1):
            for block in blocks(low - k, high + k):
                new = operator(z_ref, k + 1, block)
                if k == 0:
                    new = [0.5 * value for value in new]
                new = [a + b for a, b in zip(new, fields(z_ref, k, block))]
                if k + 2 < TERMS:
                    new = [a + b for a, b in zip(new, fields(z_ref, k + 2, block))]
                store(z_ref, k, block, new)

    chebyshev(2, 101)
    mid(
        [(24 + 8 * n, None, [(24 + 8 * n, 1 if n == 0 else 0, 7 if n == 6 else 8, False)]) for n in range(7)]
        + [(10, 78, [(10, 1, 8, False), (78, 1, 8, True)]), (18, 86, [(18, 0, 7, False), (86, 0, 7, True)])]
    )
    clenshaw(19, 84)
    for block in range(2, 11):
        at = rows(block)
        t_ref[:, at, :] = z_ref[0, :, at, :]
        p_ref[0, :, at, :] = p_ref[0, :, at, :] + STEP * z_ref[0, :, at, :]
    chebyshev(19, 84)
    mid(
        [
            (24, 48, [(24, 0, 8, False), (48, 4, 8, True)]),
            (32, 56, [(32, 0, 8, False), (56, 0, 8, True)]),
            (40, 64, [(40, 0, 8, False), (64, 0, 8, True)]),
            (48, 72, [(48, 0, 4, False), (72, 0, 8, True)]),
        ]
    )
    clenshaw(36, 67)
    at = slice(PAD + BASE, PAD + BASE + TILE)
    tendency = 0.5 * (t_ref[:, at, :] + z_ref[0, :, at, :])
    lanes = lax.broadcasted_iota(jnp.int32, (TILE, LANES), 1)
    parts = [pltpu.roll(tendency[f], (TILE * f - LEFT) % LANES, 1) for f in range(3)]
    out_ref[...] = jnp.where(lanes < TILE, parts[0], jnp.where(lanes < 2 * TILE, parts[1], parts[2]))


def vmem():
    return pl.BlockSpec(memory_space=pltpu.VMEM)


def smem():
    return pl.BlockSpec(memory_space=pltpu.SMEM)


def pack(row, times, weights, cor, state, depth):
    grid = pltpu.PrefetchScalarGridSpec(
        num_scalar_prefetch=1,
        grid=(1,),
        in_specs=[
            vmem(), vmem(), smem(), vmem(),
            pl.BlockSpec((8, NLON), lambda i, at: (lax.div(at[0], 8), 0)),
            vmem(),
        ],
        out_specs=vmem(),
        scratch_shapes=[pltpu.VMEM((8, LANES), f32)],
    )
    return pl.pallas_call(
        pack_kernel,
        out_shape=jax.ShapeDtypeStruct((2 * TILE * 4, LANES), f32),
        grid_spec=grid,
        name="pack",
    )(row, times.reshape(1, 1), weights.reshape(1, 1), cor, state, depth, jnp.asarray(series_table()))


def tile(place, own, near, far):
    return pl.pallas_call(
        tile_kernel,
        out_shape=jax.ShapeDtypeStruct((TILE, LANES), f32),
        in_specs=[smem()] + [vmem()] * 3,
        out_specs=vmem(),
        scratch_shapes=[
            pltpu.VMEM((TERMS + 1, 3, ROWS, LANES), f32),
            pltpu.VMEM((TERMS, 3, ROWS, LANES), f32),
            pltpu.VMEM((SAMPLES, SENT // LANES, W_ROWS, LANES), f32),
            pltpu.VMEM((BLOCKS, SAMPLES // 2, 16, WIDE), bf16),
            pltpu.VMEM((BLOCKS, SAMPLES // 2, 16, WIDE), bf16),
            pltpu.VMEM((3, ROWS, LANES), f32),
            pltpu.VMEM((ROWS, LANES), f32),
            pltpu.VMEM((ROWS, LANES), f32),
            pltpu.VMEM((ROWS, LANES), f32),
            pltpu.VMEM((256, 256), bf16),
            pltpu.VMEM((80, 768), bf16),
        ],
        compiler_params=pltpu.CompilerParams(vmem_limit_bytes=48 * 1024 * 1024),
        name="tile",
    )(place, own, near, far)


def unpack(columns, state):
    shape = jax.ShapeDtypeStruct((3, 8, LANES), f32)
    return pl.pallas_call(
        unpack_kernel,
        out_shape=(shape, shape),
        in_specs=[vmem(), vmem()],
        out_specs=(vmem(), vmem()),
        name="unpack",
    )(columns, state)


def per_device(ring, state_now, ocean_depth, coriolis, phase_times, phase_weights):
    state = state_now.reshape(3, 8, LANES)
    row = lax.axis_index("phase").astype(jnp.int32)
    core = lax.axis_index("core").astype(jnp.int32)
    lat = 2 * lax.axis_index("ring").astype(jnp.int32) + core
    message = pack(row[None], phase_times, phase_weights, coriolis, state, ocean_depth)
    own = lax.all_to_all(message, ("core", "phase"), 0, 0, tiled=True)
    devices = ("phase", "ring", "core")
    moves = [(at, at + 1, 0) for at in range(ring - 1)] + [(at + 1, at, 1) for at in range(ring - 1)]
    pairs = [((p * ring + a) * 2 + c, (p * ring + b) * 2 + c) for p in range(TILE) for a, b, c in moves]
    near = lax.dynamic_slice_in_dim(own, jnp.where(core == 0, 4 * (TILE - 2), 0), 4 * (TILE + 2), 0)
    near = lax.ppermute(near, devices, pairs)
    far = lax.dynamic_slice_in_dim(near, jnp.where(core == 0, 4 * TILE, 0), 8, 0)
    far = lax.ppermute(far, "core", [(0, 1), (1, 0)])
    columns = tile(lat[None], own, near, far)
    columns = lax.all_to_all(columns, "phase", 0, 0, tiled=True)
    state_next, tendency = unpack(columns, state)
    return state_next.reshape(state_now.shape), tendency.reshape(state_now.shape)


def solution(mesh):
    phase, lat = mesh.shape["phase"], mesh.shape["lat"]
    mesh = jax.sharding.Mesh(mesh.devices.reshape(phase, lat // 2, 2), ("phase", "ring", "core"))
    rows = P(None, ("ring", "core", "phase"), None)
    return jax.shard_map(
        functools.partial(per_device, lat // 2),
        mesh=mesh,
        in_specs=(rows, P(("ring", "core"), None), P(("ring", "core")), P("phase"), P("phase")),
        out_specs=(rows, rows),
        check_vma=False,
    )
```

```python
import functools
import math

import jax
import jax.numpy as jnp
import numpy as np
from jax import lax
from jax.experimental import pallas as pl
from jax.experimental.pallas import tpu as pltpu
from jax.sharding import PartitionSpec as P

DEG = 8
TERMS = DEG + 1
SERIES = 20
SCALE = 2.5
STEP = 0.5
NLON = 1024

TILE = 32
LANES = 128
LEFT = 48
BASE = 36
BLOCKS = 13
PAD = 8
ROWS = PAD + 8 * BLOCKS + PAD
WIDE = 3 * LANES
EXTRA = False
PIPELINED = True
SENT = 5 * LANES if EXTRA else WIDE
W_ROWS = 8 * 9 + 16
TILE_SHAPES = [(256, 128), (136, 128), (8, 128)]
SAMPLES = 32

f32 = jnp.float32
bf16 = jnp.bfloat16


def series_table():
    table = np.zeros((24, LANES), np.float32)
    for m in range(SERIES):
        for k in range(TERMS):
            table[m, k] = (-1.0) ** m / (math.factorial(m) * math.factorial(m + k))
    return table


def pack_kernel(row_ref, time_ref, weight_ref, cor_ref, state_ref, depth_ref, table_ref, out_ref, line_ref):
    row = row_ref[0]
    lane = lax.broadcasted_iota(jnp.int32, (1, LANES), 1)
    half = jnp.broadcast_to(time_ref[...] * 0.5, (1, LANES))
    square = half * half
    total = jnp.zeros((1, LANES), f32)
    power = jnp.ones((1, LANES), f32)
    for m in range(SERIES):
        total = total + table_ref[m : m + 1, :] * power
        power = power * square
    scale = jnp.ones((1, LANES), f32)
    for k in range(1, TERMS):
        scale = jnp.where((lane >= k) & (lane < TERMS), scale * half, scale)
    forward = total * scale
    forward = jnp.where(lane == 0, forward, 2.0 * forward)
    backward = jnp.where(lane % 2 == 0, forward, -forward) * jnp.broadcast_to(weight_ref[...], (1, LANES))
    cor = jnp.full((1, LANES), cor_ref[row], f32)
    lanes = lax.broadcasted_iota(jnp.int32, (8, LANES), 1)
    mine = lax.broadcasted_iota(jnp.int32, (8, LANES), 0) == lax.rem(row, 8)
    for q in range(8):
        depth = depth_ref[:, q * LANES : (q + 1) * LANES]
        line_ref[q : q + 1, :] = jnp.sum(jnp.where(mine, depth, 0.0), axis=0, keepdims=True)
    extras = (forward, backward, None, cor)
    for f in range(4):
        here = state_ref[f] if f < 3 else line_ref[...]
        after = pltpu.roll(here, 7, 0)
        before = pltpu.roll(here, 1, 0)
        for c in range(4):
            start = TILE * c - LEFT
            first, second = (before, here) if start < 0 else (here, after)
            shift = start % LANES
            window = jnp.where(
                lanes < LANES - shift,
                pltpu.roll(first, LANES - shift, 1),
                pltpu.roll(second, LANES - shift, 1),
            )
            if extras[f] is not None:
                window = jnp.where(lanes < TERMS, jnp.broadcast_to(extras[f], (8, LANES)), window)
            for core in range(2):
                out_ref[pl.ds(4 * (TILE * core + c) + f, 8, stride=16), :] = window


def unpack_kernel(in_ref, state_ref, next_ref, tendency_ref):
    lanes = lax.broadcasted_iota(jnp.int32, (8, LANES), 1)
    for f in range(3):
        line = jnp.zeros((8, LANES), f32)
        for c in range(4):
            piece = in_ref[pl.ds(c, 8, stride=4), :]
            shift = (TILE * (c - f)) % LANES
            if shift:
                piece = pltpu.roll(piece, shift, 1)
            line = jnp.where((lanes >= TILE * c) & (lanes < TILE * (c + 1)), piece, line)
        tendency_ref[f] = line
        next_ref[f] = state_ref[f] + STEP * line


def split(value):
    high = value.astype(bf16)
    return high, (value - high.astype(f32)).astype(bf16)


def matrices_kernel(own_ref, forward_ref, back_ref):
    term = lax.broadcasted_iota(jnp.int32, (LANES, 256), 0)
    column = lax.broadcasted_iota(jnp.int32, (LANES, 256), 1)
    group = column // 8
    high_at = (group == term) | (group - 10 == term)
    low_at = group - 20 == term
    pick_high = jnp.where(high_at & (term < TERMS), 1.0, 0.0).astype(bf16)
    pick_low = jnp.where(low_at & (term < TERMS), 1.0, 0.0).astype(bf16)
    same = lax.broadcasted_iota(jnp.int32, (256, 256), 0) % 8 == lax.broadcasted_iota(jnp.int32, (256, 256), 1) % 8

    def spread(block):
        value = own_ref[pl.ds(block, SAMPLES, stride=4), :]
        return split(jnp.broadcast_to(value[:, None, :], (SAMPLES, 8, LANES)).reshape(256, LANES))

    def picked(value, pick):
        return jnp.dot(value, pick, preferred_element_type=f32)

    high, low = spread(0)
    forward = picked(high, pick_high) + picked(low, pick_low)
    forward_ref[...] = jnp.where(same, forward, 0.0).astype(bf16)
    high, low = spread(1)
    line = lax.broadcasted_iota(jnp.int32, (80, LANES), 0) // 8
    term = lax.broadcasted_iota(jnp.int32, (80, LANES), 1)
    pick = jnp.where((line == term) & (term < TERMS), -0.5, 0.0).astype(bf16)

    def turned(value):
        value = lax.dot_general(pick, value, (((1,), (1,)), ((), ())), preferred_element_type=f32)
        return jnp.where(same[:80], value, 0.0).astype(bf16)

    back_high = turned(high)
    back_ref[:, 0:256] = back_high
    back_ref[:, 256:512] = turned(low)
    back_ref[:, 512:768] = back_high


def tile_kernel(
    place_ref, own_ref, near_ref, far_ref, forward_ref, back_ref, out_ref,
    p_ref, z_ref, w_ref, yh_ref, yl_ref, t_ref, depth_ref, cor_ref, mask_ref,
):
    lat = place_ref[0]
    core = lax.rem(lat, 2)

    def rows(block, offset=0, count=1):
        start = PAD + 8 * block + offset
        return slice(start, start + 8 * count)

    edge = jnp.zeros((3, PAD + 8, LANES), f32)
    for k in range(TERMS):
        p_ref[k, :, 0 : PAD + 8, :] = edge
        p_ref[k, :, ROWS - PAD - 8 : ROWS, :] = edge
        z_ref[k, :, PAD : PAD + 16, :] = edge
        z_ref[k, :, ROWS - PAD - 16 : ROWS - PAD, :] = edge
    p_ref[TERMS] = jnp.zeros((3, ROWS, LANES), f32)
    for s in range(SAMPLES):
        w_ref[s, :, 0:8, :] = edge[:, :8] if not EXTRA else jnp.zeros((5, 8, LANES), f32)
        w_ref[s, :, W_ROWS - 8 : W_ROWS, :] = edge[:, :8] if not EXTRA else jnp.zeros((5, 8, LANES), f32)
    for ref in (depth_ref, cor_ref):
        ref[0 : PAD + 8, :] = jnp.zeros((PAD + 8, LANES), f32)
        ref[ROWS - PAD - 8 : ROWS, :] = jnp.zeros((PAD + 8, LANES), f32)

    def place(ref, count, at):
        at = PAD + BASE + at
        h, u, v, depth, = [ref[pl.ds(f, count, stride=4), :] for f in range(4)]
        p_ref[0, 0, at : at + count, :] = h
        p_ref[0, 1, at : at + count, :] = u
        p_ref[0, 2, at : at + count, :] = v
        depth_ref[at : at + count, :] = depth * 0.4
        cor_ref[at : at + count, :] = jnp.broadcast_to(depth[:, 0:1] * 0.8, (count, LANES))

    @pl.when(core == 0)
    def _():
        place(own_ref, 2 * TILE, 0)
        place(near_ref, TILE + 2, -TILE - 2)
        place(far_ref, 2, 2 * TILE)

    @pl.when(core == 1)
    def _():
        place(own_ref, 2 * TILE, -TILE)
        place(near_ref, TILE + 2, TILE)
        place(far_ref, 2, -TILE - 2)

    at_row = lax.broadcasted_iota(jnp.int32, (ROWS, LANES), 0) + (TILE * lat - BASE - PAD)
    mask_ref[...] = jnp.where((at_row >= 0) & (at_row < 8 * TILE), 1.0, 0.0).astype(f32)

    def east(value):
        return pltpu.roll(value, LANES - 1, 1) - pltpu.roll(value, 1, 1)

    def operator(ref, k, block):
        mid, up, down = rows(block), rows(block, 1), rows(block, -1)
        h, u, v = ref[k, 0, mid, :], ref[k, 1, mid, :], ref[k, 2, mid, :]
        mask, cor = mask_ref[mid, :], cor_ref[mid, :]
        flux = east(depth_ref[mid, :] * u) + (depth_ref[up, :] * ref[k, 2, up, :] - depth_ref[down, :] * ref[k, 2, down, :])
        out_h = -(mask * flux)
        out_u = cor * v - 0.4 * east(h)
        out_v = mask * (-0.4 * (ref[k, 0, up, :] - ref[k, 0, down, :])) - cor * u
        return out_h, out_u, out_v

    def fields(ref, k, block):
        return [ref[k, f, rows(block), :] for f in range(3)]

    def store(ref, k, block, values):
        for f in range(3):
            ref[k, f, rows(block), :] = values[f]

    centre = lax.broadcasted_iota(jnp.int32, (8, LANES), 1)
    centre = (centre >= LANES // 4) & (centre < 3 * LANES // 4)

    def blocks(low, high):
        return range(low // 8, high // 8 + 1)

    def chebyshev(low, high):
        for k in range(1, TERMS):
            for block in blocks(low + k, high - k):
                new = operator(p_ref, k - 1, block)
                if k == 1:
                    new = [0.5 * value for value in new]
                else:
                    new = [a + b for a, b in zip(new, fields(p_ref, k - 2, block))]
                store(p_ref, k, block, new)

    def terms_at(f, row):
        return p_ref[:, f, PAD + row : PAD + row + 8, :].reshape(80, LANES)

    def wave(n, left, right):
        values = [terms_at(f, left) for f in range(3)]
        if right is not None:
            inside = jnp.concatenate([centre] * 10, axis=0)
            for f in range(3):
                values[f] = jnp.where(inside, values[f], pltpu.roll(terms_at(f, right), LANES // 2, 1))
        if EXTRA:
            values = values + [east(values[1]), east(values[2])]
        high, low = split(jnp.concatenate(values, axis=1))
        stacked = jnp.concatenate([high, low, high, jnp.zeros((16, SENT), bf16)], axis=0)
        waves = jnp.dot(forward_ref[...], stacked, preferred_element_type=f32)
        for f in range(len(values)):
            w_ref[:, f, 8 + 8 * n : 16 + 8 * n, :] = waves[:, f * LANES : (f + 1) * LANES].reshape(SAMPLES, 8, LANES)

    def advect(s, n):
        def at(f, offset=0):
            return w_ref[s, f, 8 + 8 * n + offset : 16 + 8 * n + offset, :]

        h, u, v = at(0), at(1), at(2)
        v_up, v_down = at(2, 1), at(2, -1)
        u_east, v_east = (at(3), at(4)) if EXTRA else (east(u), east(v))
        out_h = east(h * u) + (at(0, 1) * v_up - at(0, -1) * v_down)
        out_u = u * u_east + v * (at(1, 1) - at(1, -1))
        out_v = u * v_east + v * (v_up - v_down)
        return out_h, out_u, out_v

    def pulled(pair, n):
        one, two = advect(2 * pair, n), advect(2 * pair + 1, n)
        for f in range(3):
            high, low = split(jnp.concatenate([one[f], two[f]], axis=0))
            yh_ref[n, pair, :, f * LANES : (f + 1) * LANES] = high
            yl_ref[n, pair, :, f * LANES : (f + 1) * LANES] = low

    def weighted(n):
        high, low = yh_ref[n].reshape(256, WIDE), yl_ref[n].reshape(256, WIDE)
        return jnp.dot(back_ref[...], jnp.concatenate([high, high, low], axis=0), preferred_element_type=f32)

    def put(total, row, first, last, turn):
        at = slice(PAD + row + first, PAD + row + last)
        mask = mask_ref[at, :]
        for k in range(TERMS):
            for f in range(3):
                value = total[8 * k : 8 * k + 8, f * LANES : (f + 1) * LANES]
                if turn:
                    value = pltpu.roll(value, LANES // 2, 1)
                value = value[first:last]
                z_ref[k, f, at, :] = value * mask if f == 0 else value

    def mid(plan):
        count = len(plan)

        def finish(n):
            total = weighted(n)
            for row, first, last, turn in plan[n][2]:
                put(total, row, first, last, turn)

        if PIPELINED:
            wave(0, *plan[0][:2])
            for n in range(count):
                if n + 1 < count:
                    wave(n + 1, *plan[n + 1][:2])
                for pair in range(SAMPLES // 2):
                    pulled(pair, n)
                if n > 0:
                    finish(n - 1)
            finish(count - 1)
        else:
            for n in range(count):
                wave(n, *plan[n][:2])

            def pairs(pair, carry):
                for n in range(count):
                    pulled(pair, n)
                return carry

            lax.fori_loop(0, SAMPLES // 2, pairs, 0)
            for n in range(count):
                finish(n)

    def clenshaw(low, high):
        for k in range(DEG - 1, -1, -1):
            for block in blocks(low - k, high + k):
                new = operator(z_ref, k + 1, block)
                if k == 0:
                    new = [0.5 * value for value in new]
                new = [a + b for a, b in zip(new, fields(z_ref, k, block))]
                if k + 2 < TERMS:
                    new = [a + b for a, b in zip(new, fields(z_ref, k + 2, block))]
                store(z_ref, k, block, new)

    chebyshev(2, 101)
    mid(
        [(24 + 8 * n, None, [(24 + 8 * n, 1 if n == 0 else 0, 7 if n == 6 else 8, False)]) for n in range(7)]
        + [(10, 78, [(10, 1, 8, False), (78, 1, 8, True)]), (18, 86, [(18, 0, 7, False), (86, 0, 7, True)])]
    )
    clenshaw(19, 84)
    for block in range(2, 11):
        at = rows(block)
        t_ref[:, at, :] = z_ref[0, :, at, :]
        p_ref[0, :, at, :] = p_ref[0, :, at, :] + STEP * z_ref[0, :, at, :]
    chebyshev(19, 84)
    mid(
        [
            (24, 48, [(24, 0, 8, False), (48, 4, 8, True)]),
            (32, 56, [(32, 0, 8, False), (56, 0, 8, True)]),
            (40, 64, [(40, 0, 8, False), (64, 0, 8, True)]),
            (48, 72, [(48, 0, 4, False), (72, 0, 8, True)]),
        ]
    )
    clenshaw(36, 67)
    at = slice(PAD + BASE, PAD + BASE + TILE)
    tendency = 0.5 * (t_ref[:, at, :] + z_ref[0, :, at, :])
    lanes = lax.broadcasted_iota(jnp.int32, (TILE, LANES), 1)
    parts = [pltpu.roll(tendency[f], (TILE * f - LEFT) % LANES, 1) for f in range(3)]
    out_ref[...] = jnp.where(lanes < TILE, parts[0], jnp.where(lanes < 2 * TILE, parts[1], parts[2]))


def vmem():
    return pl.BlockSpec(memory_space=pltpu.VMEM)


def smem():
    return pl.BlockSpec(memory_space=pltpu.SMEM)


def pack(row, times, weights, cor, state, depth):
    grid = pltpu.PrefetchScalarGridSpec(
        num_scalar_prefetch=1,
        grid=(1,),
        in_specs=[
            vmem(), vmem(), smem(), vmem(),
            pl.BlockSpec((8, NLON), lambda i, at: (lax.div(at[0], 8), 0)),
            vmem(),
        ],
        out_specs=vmem(),
        scratch_shapes=[pltpu.VMEM((8, LANES), f32)],
    )
    return pl.pallas_call(
        pack_kernel,
        out_shape=jax.ShapeDtypeStruct((2 * TILE * 4, LANES), f32),
        grid_spec=grid,
        name="pack",
    )(row, times.reshape(1, 1), weights.reshape(1, 1), cor, state, depth, jnp.asarray(series_table()))


def matrices(own):
    return pl.pallas_call(
        matrices_kernel,
        out_shape=(jax.ShapeDtypeStruct((256, 256), bf16), jax.ShapeDtypeStruct((80, 768), bf16)),
        in_specs=[vmem()],
        out_specs=(vmem(), vmem()),
        cost_estimate=pl.CostEstimate(flops=60_000_000, bytes_accessed=400_000, transcendentals=0),
        name="matrices",
    )(own)


def tile(place, own, near, far, forward, back):
    return pl.pallas_call(
        tile_kernel,
        out_shape=jax.ShapeDtypeStruct((TILE, LANES), f32),
        in_specs=[smem()] + [vmem()] * 5,
        out_specs=vmem(),
        scratch_shapes=[
            pltpu.VMEM((TERMS + 1, 3, ROWS, LANES), f32),
            pltpu.VMEM((TERMS, 3, ROWS, LANES), f32),
            pltpu.VMEM((SAMPLES, SENT // LANES, W_ROWS, LANES), f32),
            pltpu.VMEM((BLOCKS, SAMPLES // 2, 16, WIDE), bf16),
            pltpu.VMEM((BLOCKS, SAMPLES // 2, 16, WIDE), bf16),
            pltpu.VMEM((3, ROWS, LANES), f32),
            pltpu.VMEM((ROWS, LANES), f32),
            pltpu.VMEM((ROWS, LANES), f32),
            pltpu.VMEM((ROWS, LANES), f32),
        ],
        compiler_params=pltpu.CompilerParams(vmem_limit_bytes=48 * 1024 * 1024),
        name="tile",
    )(place, own, near, far, forward, back)


def unpack(columns, state):
    shape = jax.ShapeDtypeStruct((3, 8, LANES), f32)
    return pl.pallas_call(
        unpack_kernel,
        out_shape=(shape, shape),
        in_specs=[vmem(), vmem()],
        out_specs=(vmem(), vmem()),
        name="unpack",
    )(columns, state)


def per_device(ring, state_now, ocean_depth, coriolis, phase_times, phase_weights):
    state = state_now.reshape(3, 8, LANES)
    row = lax.axis_index("phase").astype(jnp.int32)
    core = lax.axis_index("core").astype(jnp.int32)
    lat = 2 * lax.axis_index("ring").astype(jnp.int32) + core
    message = pack(row[None], phase_times, phase_weights, coriolis, state, ocean_depth)
    own = lax.all_to_all(message, ("core", "phase"), 0, 0, tiled=True)
    devices = ("phase", "ring", "core")
    moves = [(at, at + 1, 0) for at in range(ring - 1)] + [(at + 1, at, 1) for at in range(ring - 1)]
    pairs = [((p * ring + a) * 2 + c, (p * ring + b) * 2 + c) for p in range(TILE) for a, b, c in moves]
    near = lax.dynamic_slice_in_dim(own, jnp.where(core == 0, 4 * (TILE - 2), 0), 4 * (TILE + 2), 0)
    near = lax.ppermute(near, devices, pairs)
    near, forward, back = lax.optimization_barrier((near, *matrices(own)))
    far = lax.dynamic_slice_in_dim(near, jnp.where(core == 0, 4 * TILE, 0), 8, 0)
    far = lax.ppermute(far, "core", [(0, 1), (1, 0)])
    columns = tile(lat[None], own, near, far, forward, back)
    columns = lax.all_to_all(columns, "phase", 0, 0, tiled=True)
    state_next, tendency = unpack(columns, state)
    return state_next.reshape(state_now.shape), tendency.reshape(state_now.shape)


def solution(mesh):
    phase, lat = mesh.shape["phase"], mesh.shape["lat"]
    mesh = jax.sharding.Mesh(mesh.devices.reshape(phase, lat // 2, 2), ("phase", "ring", "core"))
    rows = P(None, ("ring", "core", "phase"), None)
    return jax.shard_map(
        functools.partial(per_device, lat // 2),
        mesh=mesh,
        in_specs=(rows, P(("ring", "core"), None), P(("ring", "core")), P("phase"), P("phase")),
        out_specs=(rows, rows),
        check_vma=False,
    )
```
